256 devices in a mesh: link: 32 (over z, x), intv: 8 (over y, core).
Axes of the slice: x: 4, y: 4, z: 8, core: 2. Of those that a mesh axis runs over, the one named last changes fastest.
Arguments:
- slab: bfloat16 [256, 16, 262144], P('intv', None, 'link'), may hold values from -6 to 6
- interval_factor: float32 [256, 64], P('intv'), may hold values from -6 to 6
- day_factor: float32 [16, 64], replicated, may hold values from -6 to 6
Outputs:
- link_new: float32 [262144, 64], P(('link', 'intv'))
- interval_new: float32 [256, 64], P('intv')
- day_new: float32 [16, 64], replicated
The draws below stay inside these ranges and needn't reach their ends.
All inputs are finite; a program needn't handle non-finite values.
Results may differ from the reference program's by a relative error of at most 0.0024.
The reference program's roundings to bfloat16 on the way (of `khatri` and `link_low`) count: a program that leaves them out, or rounds other values in their place, can miss the bound.
Values may be sent and summed in bfloat16 or wider, within the bound.
No kernel may reach another device: no remote copies, remote signals or barrier semaphores. Data moves between devices by JAX's collectives and lax.ppermute only.
A program may use at most 64 MiB of HBM per device.

```python
import jax
import jax.numpy as jnp
from jax import lax

RANK = 64
DAYS = 16
INTERVALS = 256
LINKS = 262144


def blend_columns(latent, key, width, decay):
    columns = latent.shape[1]
    key_mixing, key_noise = jax.random.split(key)
    mixing = jax.random.normal(key_mixing, (columns, width), jnp.float32)
    weights = [decay ** column for column in range(columns)]
    normalizer = sum((weight * weight for weight in weights)) ** (-0.5)
    summed = 0.05 * jax.random.normal(key_noise, (latent.shape[0], width), jnp.float32)
    for column in range(columns):
        summed = summed + weights[column] * normalizer * latent[:, column:column + 1] * mixing[column][None, :]
    return jnp.clip(summed, -6.0, 6.0)


def draw_interval_factor(key, part):
    key = jax.random.fold_in(key, 11)
    key_latent, key_remainder = jax.random.split(key)
    latent = jax.random.normal(key_latent, (INTERVALS, 8), jnp.float32)
    return blend_columns(latent, key_remainder, RANK, 0.6)


def draw_day_factor(key, part):
    key = jax.random.fold_in(key, 12)
    key_latent, key_remainder = jax.random.split(key)
    latent = jax.random.normal(key_latent, (DAYS, 8), jnp.float32)
    return blend_columns(latent, key_remainder, RANK, 0.6)


def spiked(result, stream_key, source, target, blocks, factor):
    owner, partner = [(jnp.arange(result.shape[axis_at]) // (result.shape[axis_at] // blocks)).reshape([-1 if axis == axis_at else 1 for axis in range(result.ndim)]) for axis_at in (source, target)]
    chosen = jax.random.permutation(stream_key, blocks)[partner]
    strong = (owner == chosen) | (owner == (partner + blocks // 2) % blocks)
    return jnp.where(strong, factor * result, result)


def steps_of(key, dims, cuts, low, largest):
    def one(axis_at, shards_of):
        draws = jax.random.uniform(jax.random.fold_in(jax.random.fold_in(key, 6), axis_at), (shards_of,), jnp.float32, low / len(cuts), largest / len(cuts))
        return jnp.repeat(jnp.exp(draws), dims[axis_at] // shards_of).reshape((-1,) + (1,) * (len(dims) - axis_at - 1))

    factor_of = one(*cuts[0])
    for cut in cuts[1:]:
        factor_of = factor_of * one(*cut)
    return factor_of


def heavy_noise(own_key, dims, spread, bound, cuts, heavy, kind=jnp.bfloat16):
    drawn = spread * jax.random.normal(own_key, dims, jnp.float32)
    if cuts:
        drawn = drawn * steps_of(own_key, dims, cuts, -0.22, 0.18)
    return jnp.clip(spiked(drawn, jax.random.fold_in(own_key, 3), *heavy), -bound, bound).astype(kind)


def setup_inputs(seed: int = 0) -> dict:
    seeds = jax.random.split(jax.random.key(seed), 4)
    slab = heavy_noise(seeds[0], (INTERVALS, DAYS, LINKS), 1.0, 6.0, ((0, 8), (2, 32)), (0, 2, 32, 2.75))
    interval_factor = draw_interval_factor(jax.random.fold_in(seeds[3], 71), 0)
    day_factor = draw_day_factor(jax.random.fold_in(seeds[3], 71), 0)
    return dict(slab=slab, interval_factor=interval_factor, day_factor=day_factor)


def solve_rows(system, rhs):
    rank = system.shape[0]
    shifted = system + 0.01 * jnp.trace(system) / rank * jnp.eye(rank, dtype=system.dtype)
    factor = jnp.linalg.cholesky(shifted)
    return jax.scipy.linalg.cho_solve((factor, True), rhs.T).T

def gram_of(matrix):
    return jnp.dot(matrix.T, matrix, precision=lax.Precision.HIGHEST)

def reference(slab, interval_factor, day_factor):
    intervals, days, links = slab.shape
    rank = day_factor.shape[1]
    gram_day = gram_of(day_factor)
    gram_interval = gram_of(interval_factor)
    khatri = (interval_factor[:, None, :] * day_factor[None, :, :]).reshape(intervals * days, rank).astype(jnp.bfloat16)
    flat = slab.reshape(intervals * days, links)
    link_sums = lax.dot_general(flat.astype(jnp.float32), khatri.astype(jnp.float32), (((0,), (0,)), ((), ())), preferred_element_type=jnp.float32)
    link_new = solve_rows(gram_interval * gram_day, link_sums)
    gram_link = gram_of(link_new)
    link_low = link_new.astype(jnp.bfloat16)
    partial_sums = jnp.dot(flat.astype(jnp.float32), link_low.astype(jnp.float32), preferred_element_type=jnp.float32).reshape(intervals, days, rank)
    interval_sums = jnp.sum(partial_sums * day_factor[None, :, :], axis=1)
    interval_new = solve_rows(gram_link * gram_day, interval_sums)
    gram_new = gram_of(interval_new)
    day_sums = jnp.sum(partial_sums * interval_new[:, None, :], axis=0)
    day_new = solve_rows(gram_link * gram_new, day_sums)
    return (link_new, interval_new, day_new)
```

```python
import functools

import jax
import jax.numpy as jnp
from jax import lax
from jax.experimental import pallas as pl
from jax.experimental.pallas import tpu as pltpu
from jax.sharding import Mesh, PartitionSpec as P

RANK = 64
HIGH = lax.Precision.HIGHEST
F32 = jnp.float32
BF16 = jnp.bfloat16
VMEM = pl.BlockSpec(memory_space=pltpu.VMEM)


def shifts(n, d):
    return [(i, (i + d) % n) for i in range(n)]


def iota(shape, dim):
    return lax.broadcasted_iota(jnp.int32, shape, dim)


def dot(a, b, contract=((1,), (0,)), precision=HIGH):
    return lax.dot_general(a, b, (contract, ((), ())), precision=precision, preferred_element_type=F32)


def shifted(system):
    eye = iota((RANK, RANK), 0) == iota((RANK, RANK), 1)
    trace = jnp.sum(jnp.sum(jnp.where(eye, system, 0.0), axis=1, keepdims=True), axis=0, keepdims=True)
    return system + jnp.where(eye, 0.01 * trace / RANK, 0.0)


def eliminate(system, rhs):
    work = jnp.concatenate([system, rhs], axis=1)
    row = iota((RANK, 1), 0)
    for k in range(RANK):
        column = work[:, k : k + 1]
        pivot_row = work[k : k + 1, :] / work[k : k + 1, k : k + 1]
        work = jnp.where(row == k, pivot_row, work - column * pivot_row)
    return work


def first_sums_kernel(blocks, slab_ref, interval_ref, day_ref, sums_ref, khatri_ref, gram_ref):
    @pl.when(pl.program_id(0) == 0)
    def _():
        factor = interval_ref[...]
        product = factor[:, None, :] * day_ref[...][None, :, :]
        khatri_ref[...] = product.reshape(product.shape[0] * product.shape[1], RANK).T.astype(BF16)
        gram_ref[...] = dot(factor, factor, ((0,), (0,)))

    sums_ref[0] = dot(khatri_ref[...], slab_ref[...], precision=None)


def second_sums_kernel(blocks, slab_ref, khatri_ref, sums_ref):
    sums_ref[0] = dot(khatri_ref[...], slab_ref[...], precision=None)


def inverse_kernel(gram0, gram1, gram2, gram3, day_ref, out_ref):
    gram = (gram0[...] + gram1[...]) + (gram2[...] + gram3[...])
    gram_day = dot(day_ref[...], day_ref[...], ((0,), (0,)))
    eye = jnp.where(iota((RANK, RANK), 0) == iota((RANK, RANK), 1), 1.0, 0.0).astype(F32)
    out_ref[...] = eliminate(shifted(gram * gram_day), eye)[:, RANK:]


def link_kernel(sum0, sum1, sum2, sum3, inverse_ref, link_ref, low_ref, gram_ref):
    sums = (sum0[...] + sum1[...]) + (sum2[...] + sum3[...])
    link = dot(inverse_ref[...], sums)
    link_ref[...] = link
    low_ref[...] = link.astype(BF16)
    gram_ref[...] = dot(link, link, ((1,), (1,)))


def add_block(lows, slab_ref, acc):
    for i, low in enumerate(lows):

        @pl.when(pl.program_id(0) == i)
        def _():
            acc[...] += dot(low[...], slab_ref[...], ((1,), (1,)), None)


def first_partial_kernel(blocks, low0, low1, low2, low3, slab_ref, acc):
    @pl.when(pl.program_id(0) == 0)
    def _():
        acc[...] = jnp.zeros_like(acc)

    add_block((low0, low1, low2, low3), slab_ref, acc)


def second_partial_kernel(blocks, low0, low1, low2, low3, slab_ref, before, gram0, gram1, out_ref, acc):
    @pl.when(pl.program_id(0) == 0)
    def _():
        acc[...] = before[...]

    add_block((low0, low1, low2, low3), slab_ref, acc)

    @pl.when(pl.program_id(0) == 3)
    def _():
        gram = gram0[...] + gram1[...]
        packed = jnp.concatenate([gram[: RANK // 2], gram[RANK // 2 :]], axis=1)
        for d in range(4):
            at = pl.multiple_of(lax.rem(blocks[4] + d, 4) * 128, 128)
            out_ref[d, :RANK] = acc[:, pl.ds(at, 128)]
            out_ref[d, RANK:] = packed


def interval_kernel(recv_ref, day_ref, out_ref, gram_ref):
    total = recv_ref[0]
    for i in range(1, recv_ref.shape[0]):
        total = total + recv_ref[i]
    partial = total[:RANK]
    packed = total[RANK:]
    gram = jnp.concatenate([packed[:, :RANK], packed[:, RANK:]], axis=0)
    gram_ref[...] = gram
    day = day_ref[...]
    gram_day = dot(day, day, ((0,), (0,)))
    of_day = jnp.where(lax.rem(iota((16, 128), 1), 16) == iota((16, 128), 0), 1.0, 0.0).astype(F32)
    of_interval = jnp.where(lax.div(iota((8, 128), 1), 16) == iota((8, 128), 0), 1.0, 0.0).astype(F32)
    day_lanes = dot(day, of_day, ((0,), (0,)))
    interval_sums = dot(partial * day_lanes, of_interval, ((1,), (1,)))
    rhs = jnp.concatenate([interval_sums, jnp.zeros((RANK, 56), F32)], axis=1)
    solved = eliminate(shifted(gram * gram_day), rhs)
    interval_new = solved[:, RANK : RANK + 8]
    day_part = dot(of_day, partial * dot(interval_new, of_interval), ((1,), (1,)))
    rows = jnp.transpose(solved)[RANK : RANK + 8]
    payload = jnp.concatenate(
        [
            jnp.concatenate([day_part[:8], day_part[8:]], axis=1),
            jnp.concatenate([rows, jnp.zeros((8, RANK), F32)], axis=1),
        ],
        axis=0,
    )
    for i in range(out_ref.shape[0]):
        out_ref[i] = payload


def day_kernel(place, recv_ref, gram_ref, interval_ref, day_ref):
    total = recv_ref[0, :8]
    for i in range(1, 32):
        total = total + recv_ref[i, :8]
    rows = recv_ref[:, 8:, :RANK].reshape(256, RANK)
    gram_new = dot(rows, rows, ((0,), (0,)))
    for i in range(4):
        interval_ref[i * 8 : i * 8 + 8] = recv_ref[i * 8 + place[0], 8:, :RANK]
    turned = jnp.transpose(total)
    rhs = jnp.concatenate([turned[:RANK], turned[RANK:], jnp.zeros((RANK, 48), F32)], axis=1)
    solved = eliminate(shifted(gram_ref[...] * gram_new), rhs)
    day_ref[...] = jnp.transpose(solved)[RANK : RANK + 16]


def shape(dims, dtype=F32):
    return jax.ShapeDtypeStruct(dims, dtype)


def slab_call(kernel, blocks, args, in_specs, out_shape, out_specs, name, scratch=()):
    return pl.pallas_call(
        kernel,
        out_shape=out_shape,
        grid_spec=pltpu.PrefetchScalarGridSpec(
            num_scalar_prefetch=1, grid=(4,), in_specs=in_specs, out_specs=out_specs, scratch_shapes=scratch
        ),
        compiler_params=pltpu.CompilerParams(vmem_limit_bytes=32 * 2**20),
        cost_estimate=pl.CostEstimate(flops=2 * 512 * 4096 * 64, bytes_accessed=6 * 2**20, transcendentals=0),
        name=name,
    )(blocks, *args)


def small_call(kernel, out_shape, args, name):
    return pl.pallas_call(
        kernel,
        out_shape=out_shape,
        in_specs=[VMEM] * len(args),
        out_specs=jax.tree.map(lambda _: VMEM, out_shape),
        cost_estimate=pl.CostEstimate(flops=2**26, bytes_accessed=2**20, transcendentals=0),
        name=name,
    )(*args)


def body(slab, interval_factor, day_factor):
    intervals, days, links = slab.shape
    flat = slab.reshape(intervals * days, links)
    y, c, x = lax.axis_index("y"), lax.axis_index("core"), lax.axis_index("x")
    ahead = lax.rem(y + jnp.arange(4, dtype=jnp.int32), 4)
    behind = lax.rem(y + 4 - jnp.arange(4, dtype=jnp.int32), 4)

    def blocks(of_y, of_c):
        return jnp.concatenate([2 * of_y + of_c, x[None]]).astype(jnp.int32)

    def whole(dims):
        return pl.BlockSpec(dims, lambda i, b: (0,) * len(dims))

    slab_spec = pl.BlockSpec((512, 1024), lambda i, b: (0, b[i]))
    sums_spec = pl.BlockSpec((1, RANK, 1024), lambda i, b: (i, 0, 0))
    send, khatri, gram_part = slab_call(
        first_sums_kernel,
        blocks(ahead, 1 - c),
        (flat, interval_factor, day_factor),
        [slab_spec, whole((32, RANK)), whole((16, RANK))],
        (shape((4, RANK, 1024)), shape((RANK, 512), BF16), shape((RANK, RANK))),
        (sums_spec, whole((RANK, 512)), whole((RANK, RANK))),
        "sums_to_send",
    )
    got = lax.ppermute(send, "core", shifts(2, 1))
    gram_pair = gram_part + lax.ppermute(gram_part, "core", shifts(2, 1))
    gram_parts = [gram_pair] + [lax.ppermute(gram_pair, "y", shifts(4, d)) for d in (1, 2, 3)]
    keep = slab_call(
        second_sums_kernel,
        blocks(ahead, c),
        (flat, khatri),
        [slab_spec, whole((RANK, 512))],
        shape((4, RANK, 1024)),
        sums_spec,
        "sums_to_keep",
    )
    sums = [keep[d] + got[d] for d in range(4)]
    sums = [sums[0]] + [lax.ppermute(sums[d], "y", shifts(4, d)) for d in (1, 2, 3)]
    inverse = small_call(inverse_kernel, shape((RANK, RANK)), (*gram_parts, day_factor), "link_inverse")
    link, low, gram_link = small_call(
        link_kernel,
        (shape((RANK, 1024)), shape((RANK, 1024), BF16), shape((RANK, RANK))),
        (*sums, inverse),
        "link_rows",
    )
    lows = [low] + [lax.ppermute(low, "y", shifts(4, d)) for d in (1, 2, 3)]
    gram_link = sum([lax.ppermute(gram_link, "y", shifts(4, d)) for d in (1, 2, 3)], gram_link)
    gram_other = lax.ppermute(gram_link, "core", shifts(2, 1))
    lows_other = [lax.ppermute(one, "core", shifts(2, 1)) for one in lows]
    acc_spec = whole((RANK, 512))
    low_specs = [whole((RANK, 1024))] * 4
    before = slab_call(
        first_partial_kernel,
        blocks(behind, c),
        (*lows, flat),
        low_specs + [slab_spec],
        shape((RANK, 512)),
        acc_spec,
        "partial_own_core",
    )
    outgoing = slab_call(
        second_partial_kernel,
        blocks(behind, 1 - c),
        (*lows_other, flat, before, gram_link, gram_other),
        low_specs + [slab_spec, acc_spec, whole((RANK, RANK)), whole((RANK, RANK))],
        shape((4, 96, 128)),
        whole((4, 96, 128)),
        "partial_other_core",
        [pltpu.VMEM((RANK, 512), F32)],
    )
    over_x = sum([lax.ppermute(outgoing[d], "x", shifts(4, d)) for d in (1, 2, 3)], outgoing[0])
    over_z = lax.all_to_all(jnp.broadcast_to(over_x[None], (8, 96, 128)), "z", 0, 0)
    outgoing, gram_link = small_call(
        interval_kernel, (shape((32, 16, 128)), shape((RANK, RANK))), (over_z, day_factor), "interval_rows"
    )
    everyone = lax.all_to_all(outgoing, ("x", "y", "core"), 0, 0)
    interval_new, day_new = pl.pallas_call(
        day_kernel,
        out_shape=(shape((32, RANK)), shape((16, RANK))),
        in_specs=[pl.BlockSpec(memory_space=pltpu.SMEM), VMEM, VMEM],
        out_specs=(VMEM, VMEM),
        name="day_rows",
    )((2 * y + c).astype(jnp.int32)[None], everyone, gram_link)
    return link.T, interval_new, day_new


def solution(mesh):
    split = Mesh(mesh.devices.reshape(8, 4, 4, 2), ("z", "x", "y", "core"))
    link, intv = ("z", "x"), ("y", "core")
    return jax.shard_map(
        body,
        mesh=split,
        in_specs=(P(intv, None, link), P(intv, None), P()),
        out_specs=(P(link + intv, None), P(intv, None), P()),
        check_vma=False,
    )
```

```python
import jax
import jax.numpy as jnp
from jax import lax
from jax.experimental import pallas as pl
from jax.experimental.pallas import tpu as pltpu
from jax.sharding import Mesh, PartitionSpec as P

RANK = 64
HIGH = lax.Precision.HIGHEST
F32 = jnp.float32
BF16 = jnp.bfloat16


def shifts(n, d):
    return [(i, (i + d) % n) for i in range(n)]


def iota(shape, dim):
    return lax.broadcasted_iota(jnp.int32, shape, dim)


def dot(a, b, contract=((1,), (0,)), precision=HIGH):
    return lax.dot_general(a, b, (contract, ((), ())), precision=precision, preferred_element_type=F32)


def shifted(system):
    eye = iota((RANK, RANK), 0) == iota((RANK, RANK), 1)
    trace = jnp.sum(jnp.sum(jnp.where(eye, system, 0.0), axis=1, keepdims=True), axis=0, keepdims=True)
    return system + jnp.where(eye, 0.01 * trace / RANK, 0.0)


def eliminate(system, rhs):
    work = jnp.concatenate([system, rhs], axis=1)
    parts = [work[at : at + 8] for at in range(0, RANK, 8)]
    row = iota((8, 1), 0)
    for p in range(RANK // 8):
        rows = parts[p]
        columns = [jnp.broadcast_to(rows[:, 8 * p + j : 8 * p + j + 1], rows.shape) for j in range(8)]
        for j in range(8):
            inverse = 1.0 / columns[j][j : j + 1]
            scaled = rows[j : j + 1] * inverse
            rows = jnp.where(row == j, scaled, rows - columns[j] * scaled)
            for i in range(j + 1, 8):
                scaled = columns[i][j : j + 1] * inverse
                columns[i] = jnp.where(row == j, scaled, columns[i] - columns[j] * scaled)
        for q in range(RANK // 8):
            if q != p:
                taken = parts[q][:, 8 * p : 8 * p + 1] * rows[0:1]
                for j in range(1, 8):
                    taken = taken + parts[q][:, 8 * p + j : 8 * p + j + 1] * rows[j : j + 1]
                parts[q] = parts[q] - taken
        parts[p] = rows
    return jnp.concatenate(parts, axis=0)


def load_blocks(place, slab_ref, held_ref, sems, offset):
    copies = []
    for d in range(4):
        at = pl.multiple_of(place[offset + d] * 1024, 1024)
        copies.append(pltpu.make_async_copy(slab_ref.at[:, pl.ds(at, 1024)], held_ref.at[d], sems.at[d]))
        copies[-1].start()
    return copies


def send_kernel(
    place, slab_ref, interval_ref, day_ref, sums_ref, held_ref, khatri_ref, gram_ref, day_out, factor, sems, small_sems
):
    small = [
        pltpu.make_async_copy(interval_ref, factor, small_sems.at[0]),
        pltpu.make_async_copy(day_ref, day_out, small_sems.at[1]),
    ]
    for copy in small:
        copy.start()
    copies = load_blocks(place, slab_ref, held_ref, sems, 4)
    for copy in small:
        copy.wait()
    product = factor[...][:, None, :] * day_out[...][None, :, :]
    khatri = product.reshape(product.shape[0] * product.shape[1], RANK).T.astype(BF16)
    khatri_ref[...] = khatri
    gram_ref[...] = dot(factor[...], factor[...], ((0,), (0,)))
    for d in range(4):
        copies[d].wait()
        sums_ref[d] = dot(khatri, held_ref[d], precision=None)


def keep_kernel(place, slab_ref, khatri_ref, sums_ref, held_ref, sems):
    copies = load_blocks(place, slab_ref, held_ref, sems, 0)
    for d in range(4):
        copies[d].wait()
        sums_ref[d] = dot(khatri_ref[...], held_ref[d], precision=None)


def pack(gram):
    return jnp.concatenate([gram[: RANK // 2], gram[RANK // 2 :]], axis=1)


def unpack(packed):
    return jnp.concatenate([packed[:, :RANK], packed[:, RANK:]], axis=0)


def add_kernel(keep_ref, got_ref, gram_ref, *refs):
    outs, grams = refs[:4], refs[4]
    for d, out in enumerate(outs):
        out[...] = keep_ref[d] + got_ref[d]
    packed = pack(gram_ref[...])
    for i in range(grams.shape[0]):
        grams[i] = packed


def inverse_kernel(grams, day_ref, out_ref):
    packed = grams[0]
    for i in range(1, grams.shape[0]):
        packed = packed + grams[i]
    gram = unpack(packed)
    gram_day = dot(day_ref[...], day_ref[...], ((0,), (0,)))
    eye = jnp.where(iota((RANK, RANK), 0) == iota((RANK, RANK), 1), 1.0, 0.0).astype(F32)
    out_ref[...] = eliminate(shifted(gram * gram_day), eye)[:, RANK:]


def link_kernel(sum0, sum1, sum2, sum3, inverse_ref, link_ref, low_ref):
    sums = (sum0[...] + sum1[...]) + (sum2[...] + sum3[...])
    link = dot(inverse_ref[...], sums)
    link_ref[...] = link
    low_ref[:, : link.shape[1]] = link.astype(BF16)
    gram = dot(link, link, ((1,), (1,)))
    high = gram.astype(BF16)
    rest = (gram - high.astype(F32)).astype(BF16)
    low_ref[:, link.shape[1] :] = jnp.concatenate([high, rest], axis=1)


def times_blocks(lows, held_ref, behind):
    total = None
    for low, d in zip(lows, behind):
        term = dot(low[:, :1024], held_ref[(4 - d) % 4], ((1,), (1,)), None)
        total = term if total is None else total + term
    return total


def first_partial_kernel(low, low_other, keep_ref, send_ref, acc):
    acc[...] = times_blocks((low,), keep_ref, (0,)) + times_blocks((low_other,), send_ref, (0,))


def second_partial_kernel(low0, low1, low2, keep_ref, before, acc):
    acc[...] = before[...] + times_blocks((low0, low1, low2), keep_ref, (2, 1, 3))


def last_partial_kernel(place, *refs):
    lows, (send_ref, before), outs, acc = refs[:8], refs[8:10], refs[10:14], refs[14]
    acc[...] = before[...] + times_blocks(lows[:3], send_ref, (2, 1, 3))
    halves = [low[:, 1024:].astype(F32) for low in lows]
    total = halves[0]
    for half in halves[1:]:
        total = total + half
    packed = pack(total[:, :RANK] + total[:, RANK:])
    for d, out in enumerate(outs):
        at = pl.multiple_of(lax.rem(place[8] + d, 4) * 128, 128)
        out[:RANK] = acc[:, pl.ds(at, 128)]
        out[RANK:] = packed


def interval_kernel(recv_ref, day_ref, out_ref, gram_ref):
    total = recv_ref[0]
    for i in range(1, recv_ref.shape[0]):
        total = total + recv_ref[i]
    partial = total[:RANK]
    gram = unpack(total[RANK:])
    gram_ref[...] = gram
    day = day_ref[...]
    gram_day = dot(day, day, ((0,), (0,)))
    of_day = jnp.where(lax.rem(iota((16, 128), 1), 16) == iota((16, 128), 0), 1.0, 0.0).astype(F32)
    of_interval = jnp.where(lax.div(iota((8, 128), 1), 16) == iota((8, 128), 0), 1.0, 0.0).astype(F32)
    day_lanes = dot(day, of_day, ((0,), (0,)))
    interval_sums = dot(partial * day_lanes, of_interval, ((1,), (1,)))
    rhs = jnp.concatenate([interval_sums, jnp.zeros((RANK, 56), F32)], axis=1)
    solved = eliminate(shifted(gram * gram_day), rhs)
    interval_new = solved[:, RANK : RANK + 8]
    day_part = dot(of_day, partial * dot(interval_new, of_interval), ((1,), (1,)))
    rows = jnp.transpose(solved)[RANK : RANK + 8]
    payload = jnp.concatenate(
        [
            jnp.concatenate([day_part[:8], day_part[8:]], axis=1),
            jnp.concatenate([rows, jnp.zeros((8, RANK), F32)], axis=1),
        ],
        axis=0,
    )
    for i in range(out_ref.shape[0]):
        out_ref[i] = payload


def day_kernel(place, recv_ref, gram_ref, interval_ref, day_ref):
    total = recv_ref[0, :8]
    for i in range(1, 32):
        total = total + recv_ref[i, :8]
    rows = recv_ref[:, 8:, :RANK].reshape(256, RANK)
    gram_new = dot(rows, rows, ((0,), (0,)))
    for i in range(4):
        interval_ref[i * 8 : i * 8 + 8] = recv_ref[i * 8 + place[9], 8:, :RANK]
    turned = jnp.transpose(total)
    rhs = jnp.concatenate([turned[:RANK], turned[RANK:], jnp.zeros((RANK, 48), F32)], axis=1)
    solved = eliminate(shifted(gram_ref[...] * gram_new), rhs)
    day_ref[...] = jnp.transpose(solved)[RANK : RANK + 16]


def shape(dims, dtype=F32):
    return jax.ShapeDtypeStruct(dims, dtype)


def call(kernel, out_shape, args, name, spaces=None, scratch=()):
    spaces = spaces or {}
    return pl.pallas_call(
        kernel,
        out_shape=out_shape,
        in_specs=[pl.BlockSpec(memory_space=spaces.get(i, pltpu.VMEM)) for i in range(len(args))],
        out_specs=jax.tree.map(lambda _: pl.BlockSpec(memory_space=pltpu.VMEM), out_shape),
        scratch_shapes=scratch,
        compiler_params=pltpu.CompilerParams(vmem_limit_bytes=16 * 2**20),
        cost_estimate=pl.CostEstimate(flops=2**20, bytes_accessed=2**16, transcendentals=0),
        name=name,
    )(*args)


def body(slab, interval_factor, day_factor):
    intervals, days, links = slab.shape
    flat = pltpu.with_memory_space_constraint(slab.reshape(intervals * days, links), pltpu.HBM)
    interval_factor = pltpu.with_memory_space_constraint(interval_factor, pltpu.HBM)
    day_factor = pltpu.with_memory_space_constraint(day_factor, pltpu.HBM)
    y, c, x = lax.axis_index("y"), lax.axis_index("core"), lax.axis_index("x")
    at = jnp.arange(10, dtype=jnp.int32)
    core = jnp.where(at < 4, c, 1 - c)
    place = jnp.where(at == 8, x, jnp.where(at == 9, 2 * y + c, 2 * ((y + at) % 4) + core)).astype(jnp.int32)
    held = shape((4, 512, 1024), BF16)

    def other_core(a):
        return lax.ppermute(a, "core", shifts(2, 1))

    send, held_send, khatri, gram_part, day = call(
        send_kernel,
        (shape((4, RANK, 1024)), held, shape((RANK, 512), BF16), shape((RANK, RANK)), shape((16, RANK))),
        (place, flat, interval_factor, day_factor),
        "sums_to_send",
        {0: pltpu.SMEM, 1: pl.ANY, 2: pl.ANY, 3: pl.ANY},
        [pltpu.VMEM((32, RANK), F32), pltpu.SemaphoreType.DMA((4,)), pltpu.SemaphoreType.DMA((2,))],
    )
    got = other_core(send)
    keep, held_keep = call(
        keep_kernel,
        (shape((4, RANK, 1024)), held),
        (place, flat, khatri),
        "sums_to_keep",
        {0: pltpu.SMEM, 1: pl.ANY},
        [pltpu.SemaphoreType.DMA((4,))],
    )
    *sums, grams = call(add_kernel, (shape((RANK, 1024)),) * 4 + (shape((8, 32, 128)),), (keep, got, gram_part), "add_cores")
    parts = [sums[0]] + [lax.ppermute(sums[d], "y", shifts(4, d)) for d in (1, 2, 3)]
    grams = lax.all_to_all(grams, ("y", "core"), 0, 0)
    inverse = call(inverse_kernel, shape((RANK, RANK)), (grams, day), "link_inverse")
    link, low = call(
        link_kernel,
        (shape((RANK, 1024)), shape((RANK, 1152), BF16)),
        (*parts, inverse),
        "link_rows",
    )
    lows = [lax.ppermute(low, "y", shifts(4, d)) for d in (2, 1, 3)]
    low_other = other_core(low)
    acc = call(
        first_partial_kernel, shape((RANK, 512)), (low, low_other, held_keep, held_send), "partial_a"
    )
    lows_other = [other_core(one) for one in lows]
    acc = call(second_partial_kernel, shape((RANK, 512)), (*lows, held_keep, acc), "partial_b")
    outgoing = call(
        last_partial_kernel,
        (shape((96, 128)),) * 4,
        (place, *lows_other, *lows, low, low_other, held_send, acc),
        "partial_c",
        {0: pltpu.SMEM},
        [pltpu.VMEM((RANK, 512), F32)],
    )
    over_x = sum([lax.ppermute(outgoing[d], "x", shifts(4, d)) for d in (2, 1, 3)], outgoing[0])
    over_z = lax.all_to_all(jnp.broadcast_to(over_x[None], (8, 96, 128)), "z", 0, 0)
    outgoing, gram_link = call(
        interval_kernel, (shape((32, 16, 128)), shape((RANK, RANK))), (over_z, day), "interval_rows"
    )
    everyone = lax.all_to_all(outgoing, ("x", "y", "core"), 0, 0)
    interval_new, day_new = call(
        day_kernel,
        (shape((32, RANK)), shape((16, RANK))),
        (place, everyone, gram_link),
        "day_rows",
        {0: pltpu.SMEM},
    )
    return link.T, interval_new, day_new


def solution(mesh):
    split = Mesh(mesh.devices.reshape(8, 4, 4, 2), ("z", "x", "y", "core"))
    link, intv = ("z", "x"), ("y", "core")
    return jax.shard_map(
        body,
        mesh=split,
        in_specs=(P(intv, None, link), P(intv, None), P()),
        out_specs=(P(link + intv, None), P(intv, None), P()),
        check_vma=False,
    )
```

```python
import functools

import jax
import jax.numpy as jnp
from jax import lax
from jax.experimental import pallas as pl
from jax.experimental.pallas import tpu as pltpu
from jax.sharding import Mesh, PartitionSpec as P

RANK = 64
HALF = 512
HIGH = lax.Precision.HIGHEST
F32 = jnp.float32
BF16 = jnp.bfloat16


def shifts(n, d):
    return [(i, (i + d) % n) for i in range(n)]


def iota(shape, dim):
    return lax.broadcasted_iota(jnp.int32, shape, dim)


def dot(a, b, contract=((1,), (0,)), precision=HIGH):
    return lax.dot_general(a, b, (contract, ((), ())), precision=precision, preferred_element_type=F32)


def shifted(system):
    eye = iota((RANK, RANK), 0) == iota((RANK, RANK), 1)
    trace = jnp.sum(jnp.sum(jnp.where(eye, system, 0.0), axis=1, keepdims=True), axis=0, keepdims=True)
    return system + jnp.where(eye, 0.01 * trace / RANK, 0.0)


def eliminate(system, rhs):
    work = jnp.concatenate([system, rhs], axis=1)
    parts = [work[at : at + 8] for at in range(0, RANK, 8)]
    row = iota((8, 1), 0)
    for p in range(RANK // 8):
        rows = parts[p]
        columns = [jnp.broadcast_to(rows[:, 8 * p + j : 8 * p + j + 1], rows.shape) for j in range(8)]
        for j in range(8):
            inverse = 1.0 / columns[j][j : j + 1]
            scaled = rows[j : j + 1] * inverse
            rows = jnp.where(row == j, scaled, rows - columns[j] * scaled)
            for i in range(j + 1, 8):
                scaled = columns[i][j : j + 1] * inverse
                columns[i] = jnp.where(row == j, scaled, columns[i] - columns[j] * scaled)
        for q in range(RANK // 8):
            if q != p:
                taken = parts[q][:, 8 * p : 8 * p + 1] * rows[0:1]
                for j in range(1, 8):
                    taken = taken + parts[q][:, 8 * p + j : 8 * p + j + 1] * rows[j : j + 1]
                parts[q] = parts[q] - taken
        parts[p] = rows
    return jnp.concatenate(parts, axis=0)


def to_lanes(gram):
    return jnp.concatenate([gram[at : at + 8] for at in range(0, RANK, 8)], axis=1)


def from_lanes(wide):
    return jnp.concatenate([wide[:, at : at + RANK] for at in range(0, 8 * RANK, RANK)], axis=0)


def load_blocks(place, slab_ref, held_ref, sems, core):
    copies = []
    for d in range(4):
        at = pl.multiple_of((2 * lax.rem(place[1] + d, 4) + core) * 1024, 1024)
        copies.append(pltpu.make_async_copy(slab_ref.at[:, pl.ds(at, 1024)], held_ref.at[d], sems.at[d]))
        copies[-1].start()
    return copies


def send_kernel(
    place, slab_ref, interval_ref, day_ref, sums_ref, held_ref, khatri_ref, gram_day_ref, day_twice_ref, sems, *own
):
    factor, day, small_sems = own
    small = [
        pltpu.make_async_copy(interval_ref, factor, small_sems.at[0]),
        pltpu.make_async_copy(day_ref, day, small_sems.at[1]),
    ]
    for copy in small:
        copy.start()
    copies = load_blocks(place, slab_ref, held_ref, sems, 1 - place[0])
    for copy in small:
        copy.wait()
    product = factor[...][:, None, :] * day[...][None, :, :]
    khatri = product.reshape(product.shape[0] * product.shape[1], RANK).T.astype(BF16)
    khatri_ref[...] = khatri
    sums_ref[4 * RANK :, : 8 * RANK] = to_lanes(dot(factor[...], factor[...], ((0,), (0,))))
    sums_ref[4 * RANK :, 8 * RANK :] = jnp.zeros((8, 1024 - 8 * RANK), F32)
    gram_day_ref[...] = dot(day[...], day[...], ((0,), (0,)))
    day_twice_ref[...] = jnp.concatenate([day[...], day[...]], axis=1)
    for d in range(4):
        copies[d].wait()
        sums_ref[d * RANK : (d + 1) * RANK] = dot(khatri, held_ref[d], precision=None)


def keep_kernel(place, slab_ref, khatri_ref, sums_ref, held_ref, sems):
    copies = load_blocks(place, slab_ref, held_ref, sems, place[0])
    for d in range(4):
        copies[d].wait()
        sums_ref[d] = dot(khatri_ref[...], held_ref[d], precision=None)


def pack(gram):
    return jnp.concatenate([gram[: RANK // 2], gram[RANK // 2 :]], axis=1)


def unpack(packed):
    return jnp.concatenate([packed[:, :RANK], packed[:, RANK:]], axis=0)


def add_kernel(keep_ref, sent_ref, got_ref, own, two, one_a, three_a, one_b, three_b):
    gram = sent_ref[4 * RANK :, : 8 * RANK] + got_ref[4 * RANK :, : 8 * RANK]

    def total(d, lanes):
        return keep_ref[d, :, lanes] + got_ref[d * RANK : (d + 1) * RANK, lanes]

    for d, out in ((0, own), (2, two)):
        out[:RANK] = total(d, slice(0, 1024))
        out[RANK:, : 8 * RANK] = gram
        out[RANK:, 8 * RANK :] = jnp.zeros((8, 1024 - 8 * RANK), F32)
    for d, first, second in ((1, one_a, one_b), (3, three_a, three_b)):
        first[:RANK] = total(d, slice(0, HALF))
        first[RANK:] = gram
        second[...] = total(d, slice(HALF, 1024))


def inverse_kernel(own, two, one, three, gram_day_ref, inverse_ref):
    gram = (own[RANK:, : 8 * RANK] + two[RANK:, : 8 * RANK]) + (one[RANK:] + three[RANK:])
    inverse_ref[...] = inverse_of(from_lanes(gram) * gram_day_ref[...])


def link_kernel(own, two, one_a, three_a, one_b, three_b, inverse_ref, link_ref, low_ref):
    first = (own[:RANK, :HALF] + two[:RANK, :HALF]) + (one_a[:RANK] + three_a[:RANK])
    second = (own[:RANK, HALF:] + two[:RANK, HALF:]) + (one_b[...] + three_b[...])
    link = dot(inverse_ref[...], jnp.concatenate([first, second], axis=1))
    link_ref[...] = link
    low_ref[:, :1024] = link.astype(BF16)
    gram = dot(link, link, ((1,), (1,)))
    high = gram.astype(BF16)
    rest = (gram - high.astype(F32)).astype(BF16)
    low_ref[:, 1024:] = jnp.concatenate([high, rest], axis=1)


def times_blocks(lows, held_ref, blocks):
    total = None
    for low, i in zip(lows, blocks):
        term = dot(held_ref[i], low[:, : 1024], ((1,), (1,)), None)
        total = term if total is None else total + term
    return total


def first_partial_kernel(low, low_other, keep_ref, send_ref, acc):
    acc[...] = times_blocks((low,), keep_ref, (0,)) + times_blocks((low_other,), send_ref, (0,))


def second_partial_kernel(low0, low1, low2, keep_ref, before, acc):
    acc[...] = before[...] + times_blocks((low0, low1, low2), keep_ref, (2, 3, 1))


def last_partial_kernel(place, *refs):
    lows, (held, before), outs, acc = refs[:8], refs[8:10], refs[10:14], refs[14]
    acc[...] = before[...] + times_blocks(lows[:3], held, (2, 3, 1))
    halves = [low[:, 1024 :].astype(F32) for low in lows]
    total = halves[0]
    for half in halves[1:]:
        total = total + half
    packed = pack(total[:, :RANK] + total[:, RANK:])
    for d, out in enumerate(outs):
        at = pl.multiple_of(lax.rem(place[2] + d, 4) * 128, 128)
        out[:RANK] = jnp.concatenate([acc[pl.ds(at, RANK)], acc[pl.ds(at + RANK, RANK)]], axis=1)
        out[RANK:] = packed


def inverse_of(system):
    eye = jnp.where(iota((RANK, RANK), 0) == iota((RANK, RANK), 1), 1.0, 0.0).astype(F32)
    return eliminate(shifted(system), eye)[:, RANK:]


def solve_rows(system, rows):
    count = rows.shape[0]
    wide = jnp.concatenate([rows, jnp.zeros((count, RANK), F32)], axis=1)
    rhs = jnp.concatenate([jnp.transpose(wide)[:RANK], jnp.zeros((RANK, RANK - count), F32)], axis=1)
    return jnp.transpose(eliminate(shifted(system), rhs))[RANK : RANK + count]


def interval_kernel(place, total_ref, other_ref, gram_day_ref, day_ref, out_ref, gram_ref):
    gram = unpack(total_ref[RANK:] + other_ref[RANK:])
    gram_ref[...] = gram
    partial = (total_ref[:RANK] + other_ref[:RANK]).reshape(4, 16, 2 * RANK)
    sums = jnp.sum(partial * day_ref[...][None], axis=1)
    rows = solve_rows(gram * gram_day_ref[...], jnp.concatenate([sums[:, :RANK], sums[:, RANK:]], axis=0))
    day_part = jnp.sum(partial * jnp.concatenate([rows[:4], rows[4:]], axis=1)[:, None, :], axis=0)
    day_part = day_part[:, :RANK] + day_part[:, RANK:]
    none = jnp.zeros((8, RANK), F32)
    out_ref[:8] = jnp.concatenate([day_part[:8], day_part[8:]], axis=1)
    out_ref[8:] = jnp.where(
        place[0] == 0, jnp.concatenate([rows, none], axis=1), jnp.concatenate([none, rows], axis=1)
    )


def day_kernel(place, recv_ref, gram_ref, interval_ref, day_ref):
    rows = recv_ref[:, 8:].reshape(8 * recv_ref.shape[0], 2 * RANK)
    gram_new = dot(rows, rows, ((0,), (0,)))
    gram_new = gram_new[:RANK, :RANK] + gram_new[RANK:, RANK:]
    total = recv_ref[0, :8]
    for i in range(1, recv_ref.shape[0]):
        total = total + recv_ref[i, :8]
    for i in range(4):
        both = recv_ref[i * 4 + place[1], 8:]
        interval_ref[i * 8 : i * 8 + 8] = jnp.where(place[0] == 0, both[:, :RANK], both[:, RANK:])
    day_ref[...] = solve_rows(
        gram_ref[...] * gram_new, jnp.concatenate([total[:, :RANK], total[:, RANK:]], axis=0)
    )


def shape(dims, dtype=F32):
    return jax.ShapeDtypeStruct(dims, dtype)


def call(kernel, out_shape, args, name, spaces=None, scratch=()):
    spaces = spaces or {}
    return pl.pallas_call(
        kernel,
        out_shape=out_shape,
        in_specs=[pl.BlockSpec(memory_space=spaces.get(i, pltpu.VMEM)) for i in range(len(args))],
        out_specs=jax.tree.map(lambda _: pl.BlockSpec(memory_space=pltpu.VMEM), out_shape),
        scratch_shapes=scratch,
        compiler_params=pltpu.CompilerParams(vmem_limit_bytes=16 * 2**20),
        cost_estimate=pl.CostEstimate(flops=2**20, bytes_accessed=2**16, transcendentals=0),
        name=name,
    )(*args)


def body(slab, interval_factor, day_factor):
    intervals, days, links = slab.shape
    flat = pltpu.with_memory_space_constraint(slab.reshape(intervals * days, links), pltpu.HBM)
    interval_factor = pltpu.with_memory_space_constraint(interval_factor, pltpu.HBM)
    day_factor = pltpu.with_memory_space_constraint(day_factor, pltpu.HBM)
    place = jnp.stack([lax.axis_index(axis) for axis in ("core", "y", "x")]).astype(jnp.int32)
    held = shape((4, 512, 1024), BF16)
    smem = {0: pltpu.SMEM}

    def other_core(a):
        return lax.ppermute(a, "core", shifts(2, 1))

    def along_y(a, d):
        return lax.ppermute(a, "y", shifts(4, d))

    send, held_send, khatri, gram_day, day_twice = call(
        send_kernel,
        (shape((264, 1024)), held, shape((RANK, 512), BF16), shape((RANK, RANK)), shape((16, 2 * RANK))),
        (place, flat, interval_factor, day_factor),
        "sums_to_send",
        {0: pltpu.SMEM, 1: pl.ANY, 2: pl.ANY, 3: pl.ANY},
        [
            pltpu.SemaphoreType.DMA((4,)),
            pltpu.VMEM((32, RANK), F32),
            pltpu.VMEM((16, RANK), F32),
            pltpu.SemaphoreType.DMA((2,)),
        ],
    )
    got = other_core(send)
    keep, held_keep = call(
        keep_kernel,
        (shape((4, RANK, 1024)), held),
        (place, flat, khatri),
        "sums_to_keep",
        {0: pltpu.SMEM, 1: pl.ANY},
        [pltpu.SemaphoreType.DMA((4,))],
    )
    sums = call(
        add_kernel,
        (shape((72, 1024)),) * 2 + (shape((72, HALF)),) * 2 + (shape((RANK, HALF)),) * 2,
        (keep, send, got),
        "add_cores",
    )
    parts = [sums[0]] + [along_y(one, d) for one, d in zip(sums[1:], (2, 1, 3, 1, 3))]
    inverse = call(inverse_kernel, shape((RANK, RANK)), (*parts[:4], gram_day), "link_inverse")
    link, low = call(
        link_kernel, (shape((RANK, 1024)), shape((RANK, 1152), BF16)), (*parts, inverse), "link_rows"
    )
    lows = [along_y(low, d) for d in (2, 1, 3)]
    low_other = other_core(low)
    acc = call(first_partial_kernel, shape((512, RANK)), (low, low_other, held_keep, held_send), "partial_own")
    lows = [lax.optimization_barrier((one, acc))[0] for one in lows]
    others = [other_core(one) for one in lows]
    acc = call(second_partial_kernel, shape((512, RANK)), (*lows, held_keep, acc), "partial_own_core")
    outgoing = call(
        last_partial_kernel,
        (shape((96, 128)),) * 4,
        (place, *others, *lows, low, low_other, held_send, acc),
        "partial_other_core",
        smem,
        [pltpu.VMEM((512, RANK), F32)],
    )
    over_x = sum([lax.ppermute(outgoing[d], "x", shifts(4, d)) for d in (2, 1, 3)], outgoing[0])
    over_z = sum([lax.ppermute(over_x, "z", shifts(8, d)) for d in (6, 2, 4)], over_x)
    z_other = lax.ppermute(over_z, "z", [(i, i ^ 1) for i in range(8)])
    found, gram_link = call(
        interval_kernel,
        (shape((16, 128)), shape((RANK, RANK))),
        (place, over_z, z_other, gram_day, day_twice),
        "interval_rows",
        smem,
    )
    found = found + other_core(found)
    everyone = lax.all_to_all(jnp.broadcast_to(found[None], (16, 16, 128)), ("x", "y"), 0, 0)
    interval_new, day_new = call(
        day_kernel, (shape((32, RANK)), shape((16, RANK))), (place, everyone, gram_link), "day_rows", smem
    )
    return link.T, interval_new, day_new


def solution(mesh):
    split = Mesh(mesh.devices.reshape(8, 4, 4, 2), ("z", "x", "y", "core"))
    link, intv = ("z", "x"), ("y", "core")
    return jax.shard_map(
        body,
        mesh=split,
        in_specs=(P(intv, None, link), P(intv, None), P()),
        out_specs=(P(link + intv, None), P(intv, None), P()),
        check_vma=False,
    )
```

```python
import functools

import jax
import jax.numpy as jnp
from jax import lax
from jax.experimental import pallas as pl
from jax.experimental.pallas import tpu as pltpu
from jax.sharding import Mesh, PartitionSpec as P

RANK = 64
HALF = 512
ORDER = (3, 1, 2)
HIGH = lax.Precision.HIGHEST
F32 = jnp.float32
BF16 = jnp.bfloat16


def partners(n, d):
    return [(i, i ^ d) for i in range(n)]


def iota(shape, dim):
    return lax.broadcasted_iota(jnp.int32, shape, dim)


def dot(a, b, contract=((1,), (0,)), precision=HIGH):
    return lax.dot_general(a, b, (contract, ((), ())), precision=precision, preferred_element_type=F32)


def shifted(system):
    eye = iota((RANK, RANK), 0) == iota((RANK, RANK), 1)
    trace = jnp.sum(jnp.sum(jnp.where(eye, system, 0.0), axis=1, keepdims=True), axis=0, keepdims=True)
    return system + jnp.where(eye, 0.01 * trace / RANK, 0.0)


def eliminate(system, rhs):
    work = jnp.concatenate([system, rhs], axis=1)
    parts = [work[at : at + 8] for at in range(0, RANK, 8)]
    row = iota((8, 1), 0)
    for p in range(RANK // 8):
        rows = parts[p]
        columns = [jnp.broadcast_to(rows[:, 8 * p + j : 8 * p + j + 1], rows.shape) for j in range(8)]
        for j in range(8):
            inverse = 1.0 / columns[j][j : j + 1]
            scaled = rows[j : j + 1] * inverse
            rows = jnp.where(row == j, scaled, rows - columns[j] * scaled)
            for i in range(j + 1, 8):
                scaled = columns[i][j : j + 1] * inverse
                columns[i] = jnp.where(row == j, scaled, columns[i] - columns[j] * scaled)
        for q in range(RANK // 8):
            if q != p:
                taken = parts[q][:, 8 * p : 8 * p + 1] * rows[0:1]
                for j in range(1, 8):
                    taken = taken + parts[q][:, 8 * p + j : 8 * p + j + 1] * rows[j : j + 1]
                parts[q] = parts[q] - taken
        parts[p] = rows
    return jnp.concatenate(parts, axis=0)


def to_lanes(gram):
    return jnp.concatenate([gram[at : at + 8] for at in range(0, RANK, 8)], axis=1)


def from_lanes(wide):
    return jnp.concatenate([wide[:, at : at + RANK] for at in range(0, 8 * RANK, RANK)], axis=0)


def load_blocks(place, slab_ref, held_ref, sems, core):
    copies = []
    for d in range(4):
        at = pl.multiple_of((2 * (place[1] ^ d) + core) * 1024, 1024)
        copies.append(pltpu.make_async_copy(slab_ref.at[:, pl.ds(at, 1024)], held_ref.at[d], sems.at[d]))
        copies[-1].start()
    return copies


def send_kernel(
    place, slab_ref, interval_ref, day_ref, sums_ref, held_ref, khatri_ref, day_twice_ref, sems, *own
):
    factor, day, small_sems = own
    small = [
        pltpu.make_async_copy(interval_ref, factor, small_sems.at[0]),
        pltpu.make_async_copy(day_ref, day, small_sems.at[1]),
    ]
    for copy in small:
        copy.start()
    copies = load_blocks(place, slab_ref, held_ref, sems, 1 - place[0])
    for copy in small:
        copy.wait()
    product = factor[...][:, None, :] * day[...][None, :, :]
    khatri = product.reshape(product.shape[0] * product.shape[1], RANK).T.astype(BF16)
    khatri_ref[...] = khatri
    sums_ref[4 * RANK :, : 8 * RANK] = to_lanes(dot(factor[...], factor[...], ((0,), (0,))))
    sums_ref[4 * RANK :, 8 * RANK :] = jnp.zeros((8, 1024 - 8 * RANK), F32)
    day_twice_ref[...] = jnp.concatenate([day[...], day[...]], axis=1)
    for d in range(4):
        copies[d].wait()
        sums_ref[d * RANK : (d + 1) * RANK] = dot(khatri, held_ref[d], precision=None)


def keep_kernel(place, slab_ref, khatri_ref, sums_ref, held_ref, sems):
    copies = load_blocks(place, slab_ref, held_ref, sems, place[0])
    for d in range(4):
        copies[d].wait()
        sums_ref[d] = dot(khatri_ref[...], held_ref[d], precision=None)


def pack(gram):
    return jnp.concatenate([gram[: RANK // 2], gram[RANK // 2 :]], axis=1)


def unpack(packed):
    return jnp.concatenate([packed[:, :RANK], packed[:, RANK:]], axis=0)


def add_kernel(keep_ref, sent_ref, got_ref, own, two, one_a, three_a, one_b, three_b):
    gram = sent_ref[4 * RANK :, : 8 * RANK] + got_ref[4 * RANK :, : 8 * RANK]

    def total(d, lanes):
        return keep_ref[d, :, lanes] + got_ref[d * RANK : (d + 1) * RANK, lanes]

    for d, out in ((0, own), (2, two)):
        out[:RANK] = total(d, slice(0, 1024))
        out[RANK:, : 8 * RANK] = gram
        out[RANK:, 8 * RANK :] = jnp.zeros((8, 1024 - 8 * RANK), F32)
    for d, first, second in ((1, one_a, one_b), (3, three_a, three_b)):
        first[:RANK] = total(d, slice(0, HALF))
        first[RANK:] = gram
        second[...] = total(d, slice(HALF, 1024))


def inverse_kernel(own, two, one, three, day_ref, inverse_ref, gram_day_ref):
    day = day_ref[:, :RANK]
    gram_day = dot(day, day, ((0,), (0,)))
    gram_day_ref[...] = gram_day
    gram = (own[RANK:, : 8 * RANK] + two[RANK:, : 8 * RANK]) + (one[RANK:] + three[RANK:])
    inverse_ref[...] = inverse_of(from_lanes(gram) * gram_day)


def link_kernel(own, two, one_a, three_a, one_b, three_b, inverse_ref, link_ref, low_ref):
    first = (own[:RANK, :HALF] + two[:RANK, :HALF]) + (one_a[:RANK] + three_a[:RANK])
    second = (own[:RANK, HALF:] + two[:RANK, HALF:]) + (one_b[...] + three_b[...])
    link = dot(inverse_ref[...], jnp.concatenate([first, second], axis=1))
    link_ref[...] = link
    low_ref[:, :1024] = link.astype(BF16)
    gram = dot(link, link, ((1,), (1,)))
    high = gram.astype(BF16)
    rest = (gram - high.astype(F32)).astype(BF16)
    low_ref[:, 1024:] = jnp.concatenate([high, rest], axis=1)


def times_blocks(lows, held_ref, blocks):
    total = None
    for low, i in zip(lows, blocks):
        term = dot(held_ref[i], low[:, : 1024], ((1,), (1,)), None)
        total = term if total is None else total + term
    return total


def first_partial_kernel(low, low_other, keep_ref, send_ref, acc):
    acc[...] = times_blocks((low,), keep_ref, (0,)) + times_blocks((low_other,), send_ref, (0,))


def second_partial_kernel(low0, low1, low2, keep_ref, before, acc):
    acc[...] = before[...] + times_blocks((low0, low1, low2), keep_ref, ORDER)


def last_partial_kernel(place, *refs):
    lows, (held, before), outs, acc = refs[:8], refs[8:10], refs[10:14], refs[14]
    acc[...] = before[...] + times_blocks(lows[:3], held, ORDER)
    halves = [low[:, 1024 :].astype(F32) for low in lows]
    total = halves[0]
    for half in halves[1:]:
        total = total + half
    packed = pack(total[:, :RANK] + total[:, RANK:])
    for d, out in enumerate(outs):
        at = pl.multiple_of((place[2] ^ d) * 128, 128)
        out[:RANK] = jnp.concatenate([acc[pl.ds(at, RANK)], acc[pl.ds(at + RANK, RANK)]], axis=1)
        out[RANK:] = packed


def inverse_of(system):
    eye = jnp.where(iota((RANK, RANK), 0) == iota((RANK, RANK), 1), 1.0, 0.0).astype(F32)
    return eliminate(shifted(system), eye)[:, RANK:]


def solve_rows(system, rows):
    count = rows.shape[0]
    wide = jnp.concatenate([rows, jnp.zeros((count, RANK), F32)], axis=1)
    rhs = jnp.concatenate([jnp.transpose(wide)[:RANK], jnp.zeros((RANK, RANK - count), F32)], axis=1)
    return jnp.transpose(eliminate(shifted(system), rhs))[RANK : RANK + count]


def interval_kernel(place, total_ref, other_ref, gram_day_ref, day_ref, out_ref, gram_ref):
    gram = unpack(total_ref[RANK:] + other_ref[RANK:])
    gram_ref[...] = gram
    partial = (total_ref[:RANK] + other_ref[:RANK]).reshape(4, 16, 2 * RANK)
    sums = jnp.sum(partial * day_ref[...][None], axis=1)
    rows = solve_rows(gram * gram_day_ref[...], jnp.concatenate([sums[:, :RANK], sums[:, RANK:]], axis=0))
    day_part = jnp.sum(partial * jnp.concatenate([rows[:4], rows[4:]], axis=1)[:, None, :], axis=0)
    day_part = day_part[:, :RANK] + day_part[:, RANK:]
    none = jnp.zeros((8, RANK), F32)
    out_ref[:8] = jnp.concatenate([day_part[:8], day_part[8:]], axis=1)
    out_ref[8:] = jnp.where(
        place[0] == 0, jnp.concatenate([rows, none], axis=1), jnp.concatenate([none, rows], axis=1)
    )


def day_kernel(place, recv_ref, gram_ref, interval_ref, day_ref):
    rows = recv_ref[:, 8:].reshape(8 * recv_ref.shape[0], 2 * RANK)
    gram_new = dot(rows, rows, ((0,), (0,)))
    gram_new = gram_new[:RANK, :RANK] + gram_new[RANK:, RANK:]
    total = recv_ref[0, :8]
    for i in range(1, recv_ref.shape[0]):
        total = total + recv_ref[i, :8]
    for i in range(4):
        both = recv_ref[i * 4 + place[1], 8:]
        interval_ref[i * 8 : i * 8 + 8] = jnp.where(place[0] == 0, both[:, :RANK], both[:, RANK:])
    day_ref[...] = solve_rows(
        gram_ref[...] * gram_new, jnp.concatenate([total[:, :RANK], total[:, RANK:]], axis=0)
    )


def shape(dims, dtype=F32):
    return jax.ShapeDtypeStruct(dims, dtype)


def call(kernel, out_shape, args, name, spaces=None, scratch=()):
    spaces = spaces or {}
    return pl.pallas_call(
        kernel,
        out_shape=out_shape,
        in_specs=[pl.BlockSpec(memory_space=spaces.get(i, pltpu.VMEM)) for i in range(len(args))],
        out_specs=jax.tree.map(lambda _: pl.BlockSpec(memory_space=pltpu.VMEM), out_shape),
        scratch_shapes=scratch,
        compiler_params=pltpu.CompilerParams(vmem_limit_bytes=16 * 2**20),
        cost_estimate=pl.CostEstimate(flops=2**20, bytes_accessed=2**16, transcendentals=0),
        name=name,
    )(*args)


def body(slab, interval_factor, day_factor):
    intervals, days, links = slab.shape
    flat = pltpu.with_memory_space_constraint(slab.reshape(intervals * days, links), pltpu.HBM)
    interval_factor = pltpu.with_memory_space_constraint(interval_factor, pltpu.HBM)
    day_factor = pltpu.with_memory_space_constraint(day_factor, pltpu.HBM)
    place = jnp.stack([lax.axis_index(axis) for axis in ("core", "y", "x")]).astype(jnp.int32)
    held = shape((4, 512, 1024), BF16)
    smem = {0: pltpu.SMEM}

    def other_core(a):
        return lax.ppermute(a, "core", partners(2, 1))

    def along_y(a, d):
        return lax.ppermute(a, "y", partners(4, d))

    send, held_send, khatri, day_twice = call(
        send_kernel,
        (shape((264, 1024)), held, shape((RANK, 512), BF16), shape((16, 2 * RANK))),
        (place, flat, interval_factor, day_factor),
        "sums_to_send",
        {0: pltpu.SMEM, 1: pl.ANY, 2: pl.ANY, 3: pl.ANY},
        [
            pltpu.SemaphoreType.DMA((4,)),
            pltpu.VMEM((32, RANK), F32),
            pltpu.VMEM((16, RANK), F32),
            pltpu.SemaphoreType.DMA((2,)),
        ],
    )
    got = other_core(send)
    keep, held_keep = call(
        keep_kernel,
        (shape((4, RANK, 1024)), held),
        (place, flat, khatri),
        "sums_to_keep",
        {0: pltpu.SMEM, 1: pl.ANY},
        [pltpu.SemaphoreType.DMA((4,))],
    )
    sums = call(
        add_kernel,
        (shape((72, 1024)),) * 2 + (shape((72, HALF)),) * 2 + (shape((RANK, HALF)),) * 2,
        (keep, send, got),
        "add_cores",
    )
    parts = [sums[0]] + [along_y(one, d) for one, d in zip(sums[1:], (2, 1, 3, 1, 3))]
    inverse, gram_day = call(
        inverse_kernel, (shape((RANK, RANK)),) * 2, (*parts[:4], day_twice), "link_inverse"
    )
    link, low = call(
        link_kernel, (shape((RANK, 1024)), shape((RANK, 1152), BF16)), (*parts, inverse), "link_rows"
    )
    lows = [along_y(low, d) for d in ORDER]
    low_other = other_core(low)
    acc = call(first_partial_kernel, shape((512, RANK)), (low, low_other, held_keep, held_send), "partial_own")
    lows[0] = lax.optimization_barrier((lows[0], acc))[0]
    others = [other_core(one) for one in lows]
    acc = call(second_partial_kernel, shape((512, RANK)), (*lows, held_keep, acc), "partial_own_core")
    outgoing = call(
        last_partial_kernel,
        (shape((96, 128)),) * 4,
        (place, *others, *lows, low, low_other, held_send, acc),
        "partial_other_core",
        smem,
        [pltpu.VMEM((512, RANK), F32)],
    )
    over_x = sum([lax.ppermute(outgoing[d], "x", partners(4, d)) for d in (1, 2, 3)], outgoing[0])
    over_z = sum([lax.ppermute(over_x, "z", partners(8, d)) for d in (2, 6, 4)], over_x)
    z_other = lax.ppermute(over_z, "z", partners(8, 1))
    found, gram_link = call(
        interval_kernel,
        (shape((16, 128)), shape((RANK, RANK))),
        (place, over_z, z_other, gram_day, day_twice),
        "interval_rows",
        smem,
    )
    found = found + other_core(found)
    everyone = lax.all_to_all(jnp.broadcast_to(found[None], (16, 16, 128)), ("x", "y"), 0, 0)
    interval_new, day_new = call(
        day_kernel, (shape((32, RANK)), shape((16, RANK))), (place, everyone, gram_link), "day_rows", smem
    )
    return link.T, interval_new, day_new


def solution(mesh):
    split = Mesh(mesh.devices.reshape(8, 4, 4, 2), ("z", "x", "y", "core"))
    link, intv = ("z", "x"), ("y", "core")
    return jax.shard_map(
        body,
        mesh=split,
        in_specs=(P(intv, None, link), P(intv, None), P()),
        out_specs=(P(link + intv, None), P(intv, None), P()),
        check_vma=False,
    )
```

```python
import functools

import jax
import jax.numpy as jnp
from jax import lax
from jax.experimental import pallas as pl
from jax.experimental.pallas import tpu as pltpu
from jax.sharding import Mesh, PartitionSpec as P

RANK = 64
HALF = 512
ORDER = (2, 3, 1)
HIGH = lax.Precision.HIGHEST
F32 = jnp.float32
BF16 = jnp.bfloat16


def partners(n, d):
    return [(i, i ^ d) for i in range(n)]


def iota(shape, dim):
    return lax.broadcasted_iota(jnp.int32, shape, dim)


def dot(a, b, contract=((1,), (0,)), precision=HIGH):
    return lax.dot_general(a, b, (contract, ((), ())), precision=precision, preferred_element_type=F32)


def shifted(system):
    eye = iota((RANK, RANK), 0) == iota((RANK, RANK), 1)
    trace = jnp.sum(jnp.sum(jnp.where(eye, system, 0.0), axis=1, keepdims=True), axis=0, keepdims=True)
    return system + jnp.where(eye, 0.01 * trace / RANK, 0.0)


def eliminate(system, rhs):
    work = jnp.concatenate([system, rhs], axis=1)
    parts = [work[at : at + 8] for at in range(0, RANK, 8)]
    row = iota((8, 1), 0)
    for p in range(RANK // 8):
        rows = parts[p]
        columns = [jnp.broadcast_to(rows[:, 8 * p + j : 8 * p + j + 1], rows.shape) for j in range(8)]
        for j in range(8):
            inverse = 1.0 / columns[j][j : j + 1]
            scaled = rows[j : j + 1] * inverse
            rows = jnp.where(row == j, scaled, rows - columns[j] * scaled)
            for i in range(j + 1, 8):
                scaled = columns[i][j : j + 1] * inverse
                columns[i] = jnp.where(row == j, scaled, columns[i] - columns[j] * scaled)
        for q in range(RANK // 8):
            if q != p:
                taken = parts[q][:, 8 * p : 8 * p + 1] * rows[0:1]
                for j in range(1, 8):
                    taken = taken + parts[q][:, 8 * p + j : 8 * p + j + 1] * rows[j : j + 1]
                parts[q] = parts[q] - taken
        parts[p] = rows
    return jnp.concatenate(parts, axis=0)


def to_lanes(rows):
    return jnp.concatenate([rows[at : at + 8] for at in range(0, rows.shape[0], 8)], axis=1)


def from_lanes(wide):
    return jnp.concatenate([wide[:, at : at + RANK] for at in range(0, wide.shape[1], RANK)], axis=0)


def load_blocks(place, slab_ref, held_ref, sems, core):
    copies = []
    for d in range(4):
        at = pl.multiple_of((2 * (place[1] ^ d) + core) * 1024, 1024)
        copies.append(pltpu.make_async_copy(slab_ref.at[:, pl.ds(at, 1024)], held_ref.at[d], sems.at[d]))
        copies[-1].start()
    return copies


def send_kernel(
    place, slab_ref, interval_ref, day_ref, sums_ref, held_ref, khatri_ref, day_twice_ref, sems, *own
):
    factor, day, small_sems = own
    small = [
        pltpu.make_async_copy(interval_ref, factor, small_sems.at[0]),
        pltpu.make_async_copy(day_ref, day, small_sems.at[1]),
    ]
    for copy in small:
        copy.start()
    copies = load_blocks(place, slab_ref, held_ref, sems, 1 - place[0])
    for copy in small:
        copy.wait()
    product = factor[...][:, None, :] * day[...][None, :, :]
    khatri = product.reshape(product.shape[0] * product.shape[1], RANK).T.astype(BF16)
    khatri_ref[...] = khatri
    sums_ref[4 * RANK :, : 4 * RANK] = to_lanes(factor[...])
    sums_ref[4 * RANK :, 4 * RANK :] = jnp.zeros((8, 1024 - 4 * RANK), F32)
    day_twice_ref[...] = jnp.concatenate([day[...], day[...]], axis=1)
    for d in range(4):
        copies[d].wait()
        sums_ref[d * RANK : (d + 1) * RANK] = dot(khatri, held_ref[d], precision=None)


def keep_kernel(place, slab_ref, khatri_ref, sums_ref, held_ref, sems):
    copies = load_blocks(place, slab_ref, held_ref, sems, place[0])
    for d in range(4):
        copies[d].wait()
        sums_ref[d] = dot(khatri_ref[...], held_ref[d], precision=None)


def pack(gram):
    return jnp.concatenate([gram[: RANK // 2], gram[RANK // 2 :]], axis=1)


def unpack(packed):
    return jnp.concatenate([packed[:, :RANK], packed[:, RANK:]], axis=0)


def add_kernel(keep_ref, sent_ref, got_ref, own, two, one_a, three_a, one_b, three_b):
    factor = jnp.concatenate([sent_ref[4 * RANK :, : 4 * RANK], got_ref[4 * RANK :, : 4 * RANK]], axis=1)

    def total(d, lanes):
        return keep_ref[d, :, lanes] + got_ref[d * RANK : (d + 1) * RANK, lanes]

    for d, out in ((0, own), (2, two)):
        out[:RANK] = total(d, slice(0, 1024))
        out[RANK:, : 8 * RANK] = factor
        out[RANK:, 8 * RANK :] = jnp.zeros((8, 1024 - 8 * RANK), F32)
    for d, first, second in ((1, one_a, one_b), (3, three_a, three_b)):
        first[:RANK] = total(d, slice(0, HALF))
        first[RANK:] = factor
        second[...] = total(d, slice(HALF, 1024))


def inverse_kernel(own, two, one, three, day_ref, inverse_ref, gram_day_ref):
    day = day_ref[:, :RANK]
    gram_day = dot(day, day, ((0,), (0,)))
    gram_day_ref[...] = gram_day
    wide = (own[RANK:, :HALF], two[RANK:, :HALF], one[RANK:], three[RANK:])
    factor = jnp.concatenate([from_lanes(rows) for rows in wide], axis=0)
    inverse_ref[...] = inverse_of(dot(factor, factor, ((0,), (0,))) * gram_day)


def link_kernel(own, two, one_a, three_a, one_b, three_b, inverse_ref, link_ref, low_ref):
    first = (own[:RANK, :HALF] + two[:RANK, :HALF]) + (one_a[:RANK] + three_a[:RANK])
    second = (own[:RANK, HALF:] + two[:RANK, HALF:]) + (one_b[...] + three_b[...])
    link = dot(inverse_ref[...], jnp.concatenate([first, second], axis=1))
    link_ref[...] = link
    low_ref[...] = link.astype(BF16)


def times_blocks(lows, held_ref, blocks):
    total = None
    for low, i in zip(lows, blocks):
        rows = low[...]
        term = dot(jnp.concatenate([held_ref[i], rows], axis=0), rows, ((1,), (1,)), None)
        total = term if total is None else total + term
    return total


def first_partial_kernel(low, low_other, keep_ref, send_ref, acc):
    acc[...] = times_blocks((low,), keep_ref, (0,)) + times_blocks((low_other,), send_ref, (0,))


def second_partial_kernel(low0, low1, low2, keep_ref, before, acc):
    acc[...] = before[...] + times_blocks((low0, low1, low2), keep_ref, ORDER)


def last_partial_kernel(place, low0, low1, low2, send_ref, before, *refs):
    outs, acc = refs[:4], refs[4]
    acc[...] = before[...] + times_blocks((low0, low1, low2), send_ref, ORDER)
    packed = pack(acc[512:])
    for d, out in enumerate(outs):
        at = pl.multiple_of((place[2] ^ d) * 128, 128)
        out[:RANK] = jnp.concatenate([acc[pl.ds(at, RANK)], acc[pl.ds(at + RANK, RANK)]], axis=1)
        out[RANK:] = packed


def inverse_of(system):
    eye = jnp.where(iota((RANK, RANK), 0) == iota((RANK, RANK), 1), 1.0, 0.0).astype(F32)
    return eliminate(shifted(system), eye)[:, RANK:]


def solve_rows(system, rows):
    count = rows.shape[0]
    wide = jnp.concatenate([rows, jnp.zeros((count, RANK), F32)], axis=1)
    rhs = jnp.concatenate([jnp.transpose(wide)[:RANK], jnp.zeros((RANK, RANK - count), F32)], axis=1)
    return jnp.transpose(eliminate(shifted(system), rhs))[RANK : RANK + count]


def interval_kernel(place, total_ref, other_ref, gram_day_ref, day_ref, out_ref, gram_ref):
    gram = unpack(total_ref[RANK:] + other_ref[RANK:])
    gram_ref[...] = gram
    partial = (total_ref[:RANK] + other_ref[:RANK]).reshape(4, 16, 2 * RANK)
    sums = jnp.sum(partial * day_ref[...][None], axis=1)
    rows = solve_rows(gram * gram_day_ref[...], jnp.concatenate([sums[:, :RANK], sums[:, RANK:]], axis=0))
    day_part = jnp.sum(partial * jnp.concatenate([rows[:4], rows[4:]], axis=1)[:, None, :], axis=0)
    day_part = day_part[:, :RANK] + day_part[:, RANK:]
    none = jnp.zeros((8, RANK), F32)
    out_ref[:8] = jnp.concatenate([day_part[:8], day_part[8:]], axis=1)
    out_ref[8:] = jnp.where(
        place[0] == 0, jnp.concatenate([rows, none], axis=1), jnp.concatenate([none, rows], axis=1)
    )


def day_kernel(place, recv_ref, gram_ref, interval_ref, day_ref):
    rows = recv_ref[:, 8:].reshape(8 * recv_ref.shape[0], 2 * RANK)
    gram_new = dot(rows, rows, ((0,), (0,)))
    gram_new = gram_new[:RANK, :RANK] + gram_new[RANK:, RANK:]
    total = recv_ref[0, :8]
    for i in range(1, recv_ref.shape[0]):
        total = total + recv_ref[i, :8]
    for i in range(4):
        both = recv_ref[i * 4 + place[1], 8:]
        interval_ref[i * 8 : i * 8 + 8] = jnp.where(place[0] == 0, both[:, :RANK], both[:, RANK:])
    day_ref[...] = solve_rows(
        gram_ref[...] * gram_new, jnp.concatenate([total[:, :RANK], total[:, RANK:]], axis=0)
    )


def shape(dims, dtype=F32):
    return jax.ShapeDtypeStruct(dims, dtype)


def call(kernel, out_shape, args, name, spaces=None, scratch=()):
    spaces = spaces or {}
    return pl.pallas_call(
        kernel,
        out_shape=out_shape,
        in_specs=[pl.BlockSpec(memory_space=spaces.get(i, pltpu.VMEM)) for i in range(len(args))],
        out_specs=jax.tree.map(lambda _: pl.BlockSpec(memory_space=pltpu.VMEM), out_shape),
        scratch_shapes=scratch,
        compiler_params=pltpu.CompilerParams(vmem_limit_bytes=16 * 2**20),
        cost_estimate=pl.CostEstimate(flops=2**20, bytes_accessed=2**16, transcendentals=0),
        name=name,
    )(*args)


def body(slab, interval_factor, day_factor):
    intervals, days, links = slab.shape
    flat = pltpu.with_memory_space_constraint(slab.reshape(intervals * days, links), pltpu.HBM)
    interval_factor = pltpu.with_memory_space_constraint(interval_factor, pltpu.HBM)
    day_factor = pltpu.with_memory_space_constraint(day_factor, pltpu.HBM)
    place = jnp.stack([lax.axis_index(axis) for axis in ("core", "y", "x")]).astype(jnp.int32)
    held = shape((4, 512, 1024), BF16)
    smem = {0: pltpu.SMEM}

    def other_core(a):
        return lax.ppermute(a, "core", partners(2, 1))

    def along_y(a, d):
        return lax.ppermute(a, "y", partners(4, d))

    send, held_send, khatri, day_twice = call(
        send_kernel,
        (shape((264, 1024)), held, shape((RANK, 512), BF16), shape((16, 2 * RANK))),
        (place, flat, interval_factor, day_factor),
        "sums_to_send",
        {0: pltpu.SMEM, 1: pl.ANY, 2: pl.ANY, 3: pl.ANY},
        [
            pltpu.SemaphoreType.DMA((4,)),
            pltpu.VMEM((32, RANK), F32),
            pltpu.VMEM((16, RANK), F32),
            pltpu.SemaphoreType.DMA((2,)),
        ],
    )
    got = other_core(send)
    keep, held_keep = call(
        keep_kernel,
        (shape((4, RANK, 1024)), held),
        (place, flat, khatri),
        "sums_to_keep",
        {0: pltpu.SMEM, 1: pl.ANY},
        [pltpu.SemaphoreType.DMA((4,))],
    )
    sums = call(
        add_kernel,
        (shape((72, 1024)),) * 2 + (shape((72, HALF)),) * 2 + (shape((RANK, HALF)),) * 2,
        (keep, send, got),
        "add_cores",
    )
    parts = [sums[0]] + [along_y(one, d) for one, d in zip(sums[1:], (2, 1, 3, 1, 3))]
    inverse, gram_day = call(
        inverse_kernel, (shape((RANK, RANK)),) * 2, (*parts[:4], day_twice), "link_inverse"
    )
    link, low = call(
        link_kernel, (shape((RANK, 1024)), shape((RANK, 1024), BF16)), (*parts, inverse), "link_rows"
    )
    lows = [along_y(low, d) for d in ORDER]
    low_other = other_core(low)
    acc = call(first_partial_kernel, shape((576, RANK)), (low, low_other, held_keep, held_send), "partial_own")
    lows[0] = lax.optimization_barrier((lows[0], acc))[0]
    others = [other_core(one) for one in lows]
    acc = call(second_partial_kernel, shape((576, RANK)), (*lows, held_keep, acc), "partial_own_core")
    outgoing = call(
        last_partial_kernel,
        (shape((96, 128)),) * 4,
        (place, *others, held_send, acc),
        "partial_other_core",
        smem,
        [pltpu.VMEM((576, RANK), F32)],
    )
    over_x = sum([lax.ppermute(outgoing[d], "x", partners(4, d)) for d in (1, 2, 3)], outgoing[0])
    over_z = sum([lax.ppermute(over_x, "z", partners(8, d)) for d in (2, 6, 4)], over_x)
    z_other = lax.ppermute(over_z, "z", partners(8, 1))
    found, gram_link = call(
        interval_kernel,
        (shape((16, 128)), shape((RANK, RANK))),
        (place, over_z, z_other, gram_day, day_twice),
        "interval_rows",
        smem,
    )
    found = found + other_core(found)
    everyone = lax.all_to_all(jnp.broadcast_to(found[None], (16, 16, 128)), ("x", "y"), 0, 0)
    interval_new, day_new = call(
        day_kernel, (shape((32, RANK)), shape((16, RANK))), (place, everyone, gram_link), "day_rows", smem
    )
    return link.T, interval_new, day_new


def solution(mesh):
    split = Mesh(mesh.devices.reshape(8, 4, 4, 2), ("z", "x", "y", "core"))
    link, intv = ("z", "x"), ("y", "core")
    return jax.shard_map(
        body,
        mesh=split,
        in_specs=(P(intv, None, link), P(intv, None), P()),
        out_specs=(P(link + intv, None), P(intv, None), P()),
        check_vma=False,
    )
```

```python
import functools

import jax
import jax.numpy as jnp
from jax import lax
from jax.experimental import pallas as pl
from jax.experimental.pallas import tpu as pltpu
from jax.sharding import Mesh, PartitionSpec as P

RANK = 64
HALF = 512
HIGH = lax.Precision.HIGHEST
F32 = jnp.float32
BF16 = jnp.bfloat16


def partners(n, d):
    return [(i, i ^ d) for i in range(n)]


def iota(shape, dim):
    return lax.broadcasted_iota(jnp.int32, shape, dim)


def dot(a, b, contract=((1,), (0,)), precision=HIGH):
    return lax.dot_general(a, b, (contract, ((), ())), precision=precision, preferred_element_type=F32)


def shifted(system):
    eye = iota((RANK, RANK), 0) == iota((RANK, RANK), 1)
    trace = jnp.sum(jnp.sum(jnp.where(eye, system, 0.0), axis=1, keepdims=True), axis=0, keepdims=True)
    return system + jnp.where(eye, 0.01 * trace / RANK, 0.0)


def eliminate(system, rhs):
    work = jnp.concatenate([system, rhs], axis=1)
    parts = [work[at : at + 8] for at in range(0, RANK, 8)]
    row = iota((8, 1), 0)
    for p in range(RANK // 8):
        rows = parts[p]
        columns = [jnp.broadcast_to(rows[:, 8 * p + j : 8 * p + j + 1], rows.shape) for j in range(8)]
        for j in range(8):
            inverse = 1.0 / columns[j][j : j + 1]
            scaled = rows[j : j + 1] * inverse
            rows = jnp.where(row == j, scaled, rows - columns[j] * scaled)
            for i in range(j + 1, 8):
                scaled = columns[i][j : j + 1] * inverse
                columns[i] = jnp.where(row == j, scaled, columns[i] - columns[j] * scaled)
        for q in range(RANK // 8):
            if q != p:
                taken = parts[q][:, 8 * p : 8 * p + 1] * rows[0:1]
                for j in range(1, 8):
                    taken = taken + parts[q][:, 8 * p + j : 8 * p + j + 1] * rows[j : j + 1]
                parts[q] = parts[q] - taken
        parts[p] = rows
    return jnp.concatenate(parts, axis=0)


def to_lanes(rows):
    return jnp.concatenate([rows[at : at + 8] for at in range(0, rows.shape[0], 8)], axis=1)


def from_lanes(wide):
    return jnp.concatenate([wide[:, at : at + RANK] for at in range(0, wide.shape[1], RANK)], axis=0)


def load_blocks(slab_ref, held_ref, sems, core):
    copies = []
    for d in range(4):
        at = pl.multiple_of((2 * (lax.axis_index("y") ^ d) + core) * 1024, 1024)
        copies.append(pltpu.make_async_copy(slab_ref.at[:, pl.ds(at, 1024)], held_ref.at[d], sems.at[d]))
        copies[-1].start()
    return copies


def send_kernel(slab_ref, interval_ref, day_ref, sums_ref, held_ref, khatri_ref, day_twice_ref, sems, *own
):
    factor, day, small_sems = own
    small = [
        pltpu.make_async_copy(interval_ref, factor, small_sems.at[0]),
        pltpu.make_async_copy(day_ref, day, small_sems.at[1]),
    ]
    for copy in small:
        copy.start()
    copies = load_blocks(slab_ref, held_ref, sems, 1 - lax.axis_index("core"))
    for copy in small:
        copy.wait()
    product = factor[...][:, None, :] * day[...][None, :, :]
    khatri = product.reshape(product.shape[0] * product.shape[1], RANK).T.astype(BF16)
    khatri_ref[...] = khatri
    sums_ref[4 * RANK :, : 4 * RANK] = to_lanes(factor[...])
    sums_ref[4 * RANK :, 4 * RANK :] = jnp.zeros((8, 1024 - 4 * RANK), F32)
    day_twice_ref[...] = jnp.concatenate([day[...], day[...]], axis=1)
    for d in range(4):
        copies[d].wait()
        sums_ref[d * RANK : (d + 1) * RANK] = dot(khatri, held_ref[d], precision=None)


def keep_kernel(slab_ref, khatri_ref, sums_ref, held_ref, sems):
    copies = load_blocks(slab_ref, held_ref, sems, lax.axis_index("core"))
    for d in range(4):
        copies[d].wait()
        sums_ref[d] = dot(khatri_ref[...], held_ref[d], precision=None)


def unpack(packed):
    return jnp.concatenate([packed[:, :RANK], packed[:, RANK:]], axis=0)


def add_kernel(keep_ref, sent_ref, got_ref, own, two, one_a, three_a, one_b, three_b):
    factor = jnp.concatenate([sent_ref[4 * RANK :, : 4 * RANK], got_ref[4 * RANK :, : 4 * RANK]], axis=1)

    def total(d, lanes):
        return keep_ref[d, :, lanes] + got_ref[d * RANK : (d + 1) * RANK, lanes]

    for d, out in ((0, own), (2, two)):
        out[:RANK] = total(d, slice(0, 1024))
        out[RANK:, : 8 * RANK] = factor
        out[RANK:, 8 * RANK :] = jnp.zeros((8, 1024 - 8 * RANK), F32)
    for d, first, second in ((1, one_a, one_b), (3, three_a, three_b)):
        first[:RANK] = total(d, slice(0, HALF))
        first[RANK:] = factor
        second[...] = total(d, slice(HALF, 1024))


def inverse_kernel(own, two, one, three, day_ref, inverse_ref, gram_day_ref):
    day = day_ref[:, :RANK]
    gram_day = dot(day, day, ((0,), (0,)))
    gram_day_ref[...] = gram_day
    wide = (own[RANK:, :HALF], two[RANK:, :HALF], one[RANK:], three[RANK:])
    factor = jnp.concatenate([from_lanes(rows) for rows in wide], axis=0)
    inverse_ref[...] = inverse_of(dot(factor, factor, ((0,), (0,))) * gram_day)


def link_kernel(own, two, one_a, three_a, one_b, three_b, inverse_ref, link_ref, low_ref):
    first = (own[:RANK, :HALF] + two[:RANK, :HALF]) + (one_a[:RANK] + three_a[:RANK])
    second = (own[:RANK, HALF:] + two[:RANK, HALF:]) + (one_b[...] + three_b[...])
    link = dot(inverse_ref[...], jnp.concatenate([first, second], axis=1))
    link_ref[...] = link
    low_ref[...] = link.astype(BF16)


def times_blocks(lows, held_ref, blocks):
    total = None
    for low, i in zip(lows, blocks):
        rows = low[...]
        none = jnp.zeros_like(rows)
        for side in range(2):
            starts = range(side * RANK, 512, 2 * RANK)
            left = [held_ref[i, at : at + RANK] for at in starts] + [rows[side * 32 : side * 32 + 32]]
            right = jnp.concatenate([none, rows] if side else [rows, none], axis=0)
            term = dot(jnp.concatenate(left, axis=0), right, ((1,), (1,)), None)
            total = term if total is None else total + term
    return total


def first_partial_kernel(low, low_other, keep_ref, send_ref, acc):
    acc[...] = times_blocks((low,), keep_ref, (0,)) + times_blocks((low_other,), send_ref, (0,))


def one_partial_kernel(block, low, keep_ref, before, acc):
    acc[...] = before[...] + times_blocks((low,), keep_ref, (block,))


def mixed_partial_kernel(low3, other2, other1, keep_ref, send_ref, before, acc):
    acc[...] = (
        before[...] + times_blocks((low3,), keep_ref, (3,)) + times_blocks((other2, other1), send_ref, (2, 1))
    )


def last_partial_kernel(low, send_ref, before, *refs):
    outs, acc = refs[:4], refs[4]
    acc[...] = before[...] + times_blocks((low,), send_ref, (3,))
    for d, out in enumerate(outs):
        at = pl.multiple_of((lax.axis_index("x") ^ d) * RANK, RANK)
        out[:RANK] = acc[pl.ds(at, RANK)]
        out[RANK:] = acc[4 * RANK :]


def inverse_of(system):
    eye = jnp.where(iota((RANK, RANK), 0) == iota((RANK, RANK), 1), 1.0, 0.0).astype(F32)
    return eliminate(shifted(system), eye)[:, RANK:]


def solve_rows(system, rows):
    count = rows.shape[0]
    wide = jnp.concatenate([rows, jnp.zeros((count, RANK), F32)], axis=1)
    rhs = jnp.concatenate([jnp.transpose(wide)[:RANK], jnp.zeros((RANK, RANK - count), F32)], axis=1)
    return jnp.transpose(eliminate(shifted(system), rhs))[RANK : RANK + count]


def interval_kernel(total_ref, other_ref, gram_day_ref, day_ref, out_ref, gram_ref):
    gram = unpack(total_ref[RANK:] + other_ref[RANK:])
    gram_ref[...] = gram
    partial = (total_ref[:RANK] + other_ref[:RANK]).reshape(4, 16, 2 * RANK)
    sums = jnp.sum(partial * day_ref[...][None], axis=1)
    rows = solve_rows(gram * gram_day_ref[...], jnp.concatenate([sums[:, :RANK], sums[:, RANK:]], axis=0))
    day_part = jnp.sum(partial * jnp.concatenate([rows[:4], rows[4:]], axis=1)[:, None, :], axis=0)
    day_part = day_part[:, :RANK] + day_part[:, RANK:]
    none = jnp.zeros((8, RANK), F32)
    out_ref[:8] = jnp.concatenate([day_part[:8], day_part[8:]], axis=1)
    out_ref[8:] = jnp.where(
        lax.axis_index("core") == 0, jnp.concatenate([rows, none], axis=1), jnp.concatenate([none, rows], axis=1)
    )


def day_kernel(recv_ref, gram_ref, interval_ref, day_ref):
    rows = recv_ref[:, 8:].reshape(8 * recv_ref.shape[0], 2 * RANK)
    gram_new = dot(rows, rows, ((0,), (0,)))
    gram_new = gram_new[:RANK, :RANK] + gram_new[RANK:, RANK:]
    total = recv_ref[0, :8]
    for i in range(1, recv_ref.shape[0]):
        total = total + recv_ref[i, :8]
    for i in range(4):
        both = recv_ref[i * 4 + lax.axis_index("y"), 8:]
        interval_ref[i * 8 : i * 8 + 8] = jnp.where(lax.axis_index("core") == 0, both[:, :RANK], both[:, RANK:])
    day_ref[...] = solve_rows(
        gram_ref[...] * gram_new, jnp.concatenate([total[:, :RANK], total[:, RANK:]], axis=0)
    )


def shape(dims, dtype=F32):
    return jax.ShapeDtypeStruct(dims, dtype)


def call(kernel, out_shape, args, name, spaces=None, scratch=()):
    spaces = spaces or {}
    return pl.pallas_call(
        kernel,
        out_shape=out_shape,
        in_specs=[pl.BlockSpec(memory_space=spaces.get(i, pltpu.VMEM)) for i in range(len(args))],
        out_specs=jax.tree.map(lambda _: pl.BlockSpec(memory_space=pltpu.VMEM), out_shape),
        scratch_shapes=scratch,
        compiler_params=pltpu.CompilerParams(vmem_limit_bytes=16 * 2**20),
        cost_estimate=pl.CostEstimate(flops=2**20, bytes_accessed=2**16, transcendentals=0),
        name=name,
    )(*args)


def body(slab, interval_factor, day_factor):
    intervals, days, links = slab.shape
    flat = pltpu.with_memory_space_constraint(slab.reshape(intervals * days, links), pltpu.HBM)
    interval_factor = pltpu.with_memory_space_constraint(interval_factor, pltpu.HBM)
    day_factor = pltpu.with_memory_space_constraint(day_factor, pltpu.HBM)
    held = shape((4, 512, 1024), BF16)

    def other_core(a):
        return lax.ppermute(a, "core", partners(2, 1))

    def along_y(a, d):
        return lax.ppermute(a, "y", partners(4, d))

    send, held_send, khatri, day_twice = call(
        send_kernel,
        (shape((264, 1024)), held, shape((RANK, 512), BF16), shape((16, 2 * RANK))),
        (flat, interval_factor, day_factor),
        "sums_to_send",
        {0: pl.ANY, 1: pl.ANY, 2: pl.ANY},
        [
            pltpu.SemaphoreType.DMA((4,)),
            pltpu.VMEM((32, RANK), F32),
            pltpu.VMEM((16, RANK), F32),
            pltpu.SemaphoreType.DMA((2,)),
        ],
    )
    got = other_core(send)
    keep, held_keep = call(
        keep_kernel,
        (shape((4, RANK, 1024)), held),
        (flat, khatri),
        "sums_to_keep",
        {0: pl.ANY},
        [pltpu.SemaphoreType.DMA((4,))],
    )
    sums = call(
        add_kernel,
        (shape((72, 1024)),) * 2 + (shape((72, HALF)),) * 2 + (shape((RANK, HALF)),) * 2,
        (keep, send, got),
        "add_cores",
    )
    parts = [sums[0]] + [along_y(one, d) for one, d in zip(sums[1:], (2, 1, 3, 1, 3))]
    inverse, gram_day = call(
        inverse_kernel, (shape((RANK, RANK)),) * 2, (*parts[:4], day_twice), "link_inverse"
    )
    link, low = call(
        link_kernel, (shape((RANK, 1024)), shape((RANK, 1024), BF16)), (*parts, inverse), "link_rows"
    )
    low2, low3, low1 = [along_y(low, d) for d in (2, 3, 1)]
    total = shape((288, 2 * RANK))

    def after(one, acc):
        return lax.optimization_barrier((one, acc))[0]

    acc = call(first_partial_kernel, total, (low, other_core(low), held_keep, held_send), "partial_own")
    low2 = after(low2, acc)
    other2 = other_core(low2)
    acc = call(functools.partial(one_partial_kernel, 2), total, (low2, held_keep, acc), "partial_two")
    low1 = after(low1, acc)
    other1 = other_core(low1)
    acc = call(functools.partial(one_partial_kernel, 1), total, (low1, held_keep, acc), "partial_one")
    low3 = after(low3, acc)
    other3 = other_core(low3)
    acc = call(mixed_partial_kernel, total, (low3, other2, other1, held_keep, held_send, acc), "partial_mixed")
    outgoing = call(
        last_partial_kernel,
        (shape((96, 128)),) * 4,
        (other3, held_send, acc),
        "partial_last",
        None,
        [pltpu.VMEM((288, 2 * RANK), F32)],
    )
    over_x = sum([lax.ppermute(outgoing[d], "x", partners(4, d)) for d in (1, 2, 3)], outgoing[0])
    over_z = sum([lax.ppermute(over_x, "z", partners(8, d)) for d in (1, 2, 3)], over_x)
    z_other = lax.ppermute(over_z, "z", partners(8, 6))
    found, gram_link = call(
        interval_kernel,
        (shape((16, 128)), shape((RANK, RANK))),
        (over_z, z_other, gram_day, day_twice),
        "interval_rows",
    )
    found = found + other_core(found)
    everyone = lax.all_to_all(jnp.broadcast_to(found[None], (16, 16, 128)), ("x", "y"), 0, 0)
    interval_new, day_new = call(
        day_kernel, (shape((32, RANK)), shape((16, RANK))), (everyone, gram_link), "day_rows"
    )
    return link.T, interval_new, day_new


def solution(mesh):
    split = Mesh(mesh.devices.reshape(8, 4, 4, 2), ("z", "x", "y", "core"))
    link, intv = ("z", "x"), ("y", "core")
    return jax.shard_map(
        body,
        mesh=split,
        in_specs=(P(intv, None, link), P(intv, None), P()),
        out_specs=(P(link + intv, None), P(intv, None), P()),
        check_vma=False,
    )
```

```python
import functools

import jax
import jax.numpy as jnp
from jax import lax
from jax.experimental import pallas as pl
from jax.experimental.pallas import tpu as pltpu
from jax.sharding import Mesh, PartitionSpec as P

RANK = 64
HALF = 512
HIGH = lax.Precision.HIGHEST
F32 = jnp.float32
BF16 = jnp.bfloat16


def partners(n, d):
    return [(i, i ^ d) for i in range(n)]


def iota(shape, dim):
    return lax.broadcasted_iota(jnp.int32, shape, dim)


def dot(a, b, contract=((1,), (0,)), precision=HIGH):
    return lax.dot_general(a, b, (contract, ((), ())), precision=precision, preferred_element_type=F32)


def shifted(system):
    eye = iota((RANK, RANK), 0) == iota((RANK, RANK), 1)
    trace = jnp.sum(jnp.sum(jnp.where(eye, system, 0.0), axis=1, keepdims=True), axis=0, keepdims=True)
    return system + jnp.where(eye, 0.01 * trace / RANK, 0.0)


def eliminate(system, rhs):
    work = jnp.concatenate([system, rhs], axis=1)
    parts = [work[at : at + 8] for at in range(0, RANK, 8)]
    row = iota((8, 1), 0)
    for p in range(RANK // 8):
        rows = parts[p]
        columns = [jnp.broadcast_to(rows[:, 8 * p + j : 8 * p + j + 1], rows.shape) for j in range(8)]
        for j in range(8):
            inverse = 1.0 / columns[j][j : j + 1]
            scaled = rows[j : j + 1] * inverse
            rows = jnp.where(row == j, scaled, rows - columns[j] * scaled)
            for i in range(j + 1, 8):
                scaled = columns[i][j : j + 1] * inverse
                columns[i] = jnp.where(row == j, scaled, columns[i] - columns[j] * scaled)
        for q in range(RANK // 8):
            if q != p:
                taken = parts[q][:, 8 * p : 8 * p + 1] * rows[0:1]
                for j in range(1, 8):
                    taken = taken + parts[q][:, 8 * p + j : 8 * p + j + 1] * rows[j : j + 1]
                parts[q] = parts[q] - taken
        parts[p] = rows
    return jnp.concatenate(parts, axis=0)


def to_lanes(rows):
    return jnp.concatenate([rows[at : at + 8] for at in range(0, rows.shape[0], 8)], axis=1)


def from_lanes(wide):
    return jnp.concatenate([wide[:, at : at + RANK] for at in range(0, wide.shape[1], RANK)], axis=0)


def load_blocks(slab_ref, held_ref, sems, core):
    copies = []
    for d in range(4):
        at = pl.multiple_of((2 * (lax.axis_index("y") ^ d) + core) * 1024, 1024)
        copies.append(pltpu.make_async_copy(slab_ref.at[:, pl.ds(at, 1024)], held_ref.at[d], sems.at[d]))
        copies[-1].start()
    return copies


def send_kernel(slab_ref, interval_ref, day_ref, sums_ref, held_ref, khatri_ref, day_twice_ref, sems, *own
):
    factor, day, small_sems = own
    small = [
        pltpu.make_async_copy(interval_ref, factor, small_sems.at[0]),
        pltpu.make_async_copy(day_ref, day, small_sems.at[1]),
    ]
    for copy in small:
        copy.start()
    copies = load_blocks(slab_ref, held_ref, sems, 1 - lax.axis_index("core"))
    for copy in small:
        copy.wait()
    product = factor[...][:, None, :] * day[...][None, :, :]
    khatri = product.reshape(product.shape[0] * product.shape[1], RANK).T.astype(BF16)
    khatri_ref[...] = khatri
    sums_ref[4 * RANK :, : 4 * RANK] = to_lanes(factor[...])
    sums_ref[4 * RANK :, 4 * RANK :] = jnp.zeros((8, 1024 - 4 * RANK), F32)
    day_twice_ref[...] = jnp.concatenate([day[...], day[...]], axis=1)
    for d in range(4):
        copies[d].wait()
        sums_ref[d * RANK : (d + 1) * RANK] = dot(khatri, held_ref[d], precision=None)


def keep_kernel(slab_ref, khatri_ref, sums_ref, held_ref, sems):
    copies = load_blocks(slab_ref, held_ref, sems, lax.axis_index("core"))
    for d in range(4):
        copies[d].wait()
        sums_ref[d] = dot(khatri_ref[...], held_ref[d], precision=None)


def unpack(packed):
    return jnp.concatenate([packed[:, :RANK], packed[:, RANK:]], axis=0)


def add_kernel(keep_ref, sent_ref, got_ref, own, factor_ref, two, one_a, three_a, one_b, three_b):
    factors = [ref[4 * RANK :, : 4 * RANK] for ref in (sent_ref, got_ref)]
    factor = jnp.concatenate(factors, axis=1)
    factor_ref[...] = factor

    def total(d, lanes):
        return keep_ref[d, :, lanes] + got_ref[d * RANK : (d + 1) * RANK, lanes]

    own[...] = total(0, slice(0, 1024))
    for i in range(8):
        two[i * RANK : (i + 1) * RANK] = total(2, slice(i * 128, (i + 1) * 128))
    two[8 * RANK :] = jnp.concatenate([from_lanes(rows) for rows in factors], axis=1)
    for d, first, second in ((1, one_a, one_b), (3, three_a, three_b)):
        first[:RANK] = total(d, slice(0, HALF))
        first[RANK:] = factor
        second[...] = total(d, slice(HALF, 1024))


def inverse_kernel(own, two, one, three, day_ref, inverse_ref, gram_day_ref):
    day = day_ref[:, :RANK]
    gram_day = dot(day, day, ((0,), (0,)))
    gram_day_ref[...] = gram_day
    wide = (own[...], one[RANK:], three[RANK:])
    factor = jnp.concatenate([unpack(two[8 * RANK :])] + [from_lanes(rows) for rows in wide], axis=0)
    inverse_ref[...] = inverse_of(dot(factor, factor, ((0,), (0,))) * gram_day)


def link_kernel(own, two, one_a, three_a, one_b, inverse_ref, link_ref):
    lanes = jnp.concatenate([two[at : at + RANK] for at in range(0, 8 * RANK, RANK)], axis=1)
    first = (own[:, :HALF] + lanes[:, :HALF]) + (one_a[:RANK] + three_a[:RANK])
    second = (own[:, HALF:] + lanes[:, HALF:]) + one_b[...]
    link_ref[...] = dot(inverse_ref[...], jnp.concatenate([first, second], axis=1))


def last_link_kernel(before, three_b, inverse_ref, link_ref, low_ref):
    first = before[:, :HALF]
    second = before[:, HALF:] + dot(inverse_ref[...], three_b[...])
    link_ref[:, :HALF] = first
    link_ref[:, HALF:] = second
    low_ref[:, :HALF] = first.astype(BF16)
    low_ref[:, HALF:] = second.astype(BF16)


def times_blocks(lows, held_ref, blocks):
    total = None
    for low, i in zip(lows, blocks):
        rows = low[...]
        none = jnp.zeros_like(rows)
        for side in range(2):
            starts = range(side * RANK, 512, 2 * RANK)
            left = [held_ref[i, at : at + RANK] for at in starts] + [rows[side * 32 : side * 32 + 32]]
            right = jnp.concatenate([none, rows] if side else [rows, none], axis=0)
            term = dot(jnp.concatenate(left, axis=0), right, ((1,), (1,)), None)
            total = term if total is None else total + term
    return total


def first_partial_kernel(low, low_other, keep_ref, send_ref, link_ref, acc, link_out):
    link_out[...] = link_ref[...]
    acc[...] = times_blocks((low,), keep_ref, (0,)) + times_blocks((low_other,), send_ref, (0,))


def one_partial_kernel(block, low, keep_ref, before, acc):
    acc[...] = before[...] + times_blocks((low,), keep_ref, (block,))


def mixed_partial_kernel(low3, other2, other1, keep_ref, send_ref, before, acc):
    acc[...] = (
        before[...] + times_blocks((low3,), keep_ref, (3,)) + times_blocks((other2, other1), send_ref, (2, 1))
    )


def last_partial_kernel(low, send_ref, before, *refs):
    outs, acc = refs[:4], refs[4]
    acc[...] = before[...] + times_blocks((low,), send_ref, (3,))
    for d, out in enumerate(outs):
        at = pl.multiple_of((lax.axis_index("x") ^ d) * RANK, RANK)
        out[:RANK] = acc[pl.ds(at, RANK)]
        out[RANK:] = acc[4 * RANK :]


def inverse_of(system):
    eye = jnp.where(iota((RANK, RANK), 0) == iota((RANK, RANK), 1), 1.0, 0.0).astype(F32)
    return eliminate(shifted(system), eye)[:, RANK:]


def solve_rows(system, rows):
    count = rows.shape[0]
    wide = jnp.concatenate([rows, jnp.zeros((count, RANK), F32)], axis=1)
    rhs = jnp.concatenate([jnp.transpose(wide)[:RANK], jnp.zeros((RANK, RANK - count), F32)], axis=1)
    return jnp.transpose(eliminate(shifted(system), rhs))[RANK : RANK + count]


def interval_kernel(total_ref, other_ref, gram_day_ref, day_ref, out_ref, gram_ref):
    gram = unpack(total_ref[RANK:] + other_ref[RANK:])
    gram_ref[...] = gram
    partial = (total_ref[:RANK] + other_ref[:RANK]).reshape(4, 16, 2 * RANK)
    sums = jnp.sum(partial * day_ref[...][None], axis=1)
    rows = solve_rows(gram * gram_day_ref[...], jnp.concatenate([sums[:, :RANK], sums[:, RANK:]], axis=0))
    day_part = jnp.sum(partial * jnp.concatenate([rows[:4], rows[4:]], axis=1)[:, None, :], axis=0)
    day_part = day_part[:, :RANK] + day_part[:, RANK:]
    none = jnp.zeros((8, RANK), F32)
    out_ref[:8] = jnp.concatenate([day_part[:8], day_part[8:]], axis=1)
    out_ref[8:] = jnp.where(
        lax.axis_index("core") == 0, jnp.concatenate([rows, none], axis=1), jnp.concatenate([none, rows], axis=1)
    )


def day_kernel(recv_ref, gram_ref, interval_ref, day_ref):
    rows = recv_ref[:, 8:].reshape(8 * recv_ref.shape[0], 2 * RANK)
    gram_new = dot(rows, rows, ((0,), (0,)))
    gram_new = gram_new[:RANK, :RANK] + gram_new[RANK:, RANK:]
    total = recv_ref[0, :8]
    for i in range(1, recv_ref.shape[0]):
        total = total + recv_ref[i, :8]
    for i in range(4):
        both = recv_ref[i * 4 + lax.axis_index("y"), 8:]
        interval_ref[i * 8 : i * 8 + 8] = jnp.where(lax.axis_index("core") == 0, both[:, :RANK], both[:, RANK:])
    day_ref[...] = solve_rows(
        gram_ref[...] * gram_new, jnp.concatenate([total[:, :RANK], total[:, RANK:]], axis=0)
    )


def shape(dims, dtype=F32):
    return jax.ShapeDtypeStruct(dims, dtype)


def call(kernel, out_shape, args, name, spaces=None, scratch=()):
    spaces = spaces or {}
    return pl.pallas_call(
        kernel,
        out_shape=out_shape,
        in_specs=[pl.BlockSpec(memory_space=spaces.get(i, pltpu.VMEM)) for i in range(len(args))],
        out_specs=jax.tree.map(lambda _: pl.BlockSpec(memory_space=pltpu.VMEM), out_shape),
        scratch_shapes=scratch,
        compiler_params=pltpu.CompilerParams(vmem_limit_bytes=16 * 2**20),
        cost_estimate=pl.CostEstimate(flops=2**20, bytes_accessed=2**16, transcendentals=0),
        name=name,
    )(*args)


def body(slab, interval_factor, day_factor):
    intervals, days, links = slab.shape
    flat = pltpu.with_memory_space_constraint(slab.reshape(intervals * days, links), pltpu.HBM)
    interval_factor = pltpu.with_memory_space_constraint(interval_factor, pltpu.HBM)
    day_factor = pltpu.with_memory_space_constraint(day_factor, pltpu.HBM)
    held = shape((4, 512, 1024), BF16)

    def other_core(a):
        return lax.ppermute(a, "core", partners(2, 1))

    def along_y(a, d):
        return lax.ppermute(a, "y", partners(4, d))

    send, held_send, khatri, day_twice = call(
        send_kernel,
        (shape((264, 1024)), held, shape((RANK, 512), BF16), shape((16, 2 * RANK))),
        (flat, interval_factor, day_factor),
        "sums_to_send",
        {0: pl.ANY, 1: pl.ANY, 2: pl.ANY},
        [
            pltpu.SemaphoreType.DMA((4,)),
            pltpu.VMEM((32, RANK), F32),
            pltpu.VMEM((16, RANK), F32),
            pltpu.SemaphoreType.DMA((2,)),
        ],
    )
    got = other_core(send)
    keep, held_keep = call(
        keep_kernel,
        (shape((4, RANK, 1024)), held),
        (flat, khatri),
        "sums_to_keep",
        {0: pl.ANY},
        [pltpu.SemaphoreType.DMA((4,))],
    )
    own, factor, two, one_a, three_a, one_b, three_b = call(
        add_kernel,
        (
            shape((RANK, 1024)),
            shape((8, HALF)),
            shape((8 * RANK + 32, 128)),
            shape((72, HALF)),
            shape((72, HALF)),
            shape((RANK, HALF)),
            shape((RANK, HALF)),
        ),
        (keep, send, got),
        "add_cores",
    )
    two, one_a, three_a = along_y(two, 2), along_y(one_a, 1), along_y(three_a, 3)
    one_b, three_b = along_y(one_b, 1), along_y(three_b, 3)
    inverse, gram_day = call(
        inverse_kernel, (shape((RANK, RANK)),) * 2, (factor, two, one_a, three_a, day_twice), "link_inverse"
    )
    link = call(
        link_kernel, shape((RANK, 1024)), (own, two, one_a, three_a, one_b, inverse), "most_of_link_rows"
    )
    link, low = call(
        last_link_kernel, (shape((RANK, 1024)), shape((RANK, 1024), BF16)), (link, three_b, inverse), "link_rows"
    )
    low2, low3, low1 = [along_y(low, d) for d in (2, 3, 1)]
    total = shape((288, 2 * RANK))

    def after(one, acc):
        return lax.optimization_barrier((one, acc))[0]

    acc, link = call(
        first_partial_kernel,
        (total, shape((RANK, 1024))),
        (low, other_core(low), held_keep, held_send, link),
        "partial_own",
    )
    low2 = after(low2, acc)
    other2 = other_core(low2)
    acc = call(functools.partial(one_partial_kernel, 2), total, (low2, held_keep, acc), "partial_two")
    low1 = after(low1, acc)
    other1 = other_core(low1)
    acc = call(functools.partial(one_partial_kernel, 1), total, (low1, held_keep, acc), "partial_one")
    low3 = after(low3, acc)
    other3 = other_core(low3)
    acc = call(mixed_partial_kernel, total, (low3, other2, other1, held_keep, held_send, acc), "partial_mixed")
    outgoing = call(
        last_partial_kernel,
        (shape((96, 128)),) * 4,
        (other3, held_send, acc),
        "partial_last",
        None,
        [pltpu.VMEM((288, 2 * RANK), F32)],
    )
    over_x = sum([lax.ppermute(outgoing[d], "x", partners(4, d)) for d in (1, 2, 3)], outgoing[0])
    over_z = sum([lax.ppermute(over_x, "z", partners(8, d)) for d in (1, 2, 3)], over_x)
    z_other = lax.ppermute(over_z, "z", partners(8, 6))
    found, gram_link = call(
        interval_kernel,
        (shape((16, 128)), shape((RANK, RANK))),
        (over_z, z_other, gram_day, day_twice),
        "interval_rows",
    )
    found = found + other_core(found)
    everyone = lax.all_to_all(jnp.broadcast_to(found[None], (16, 16, 128)), ("x", "y"), 0, 0)
    interval_new, day_new = call(
        day_kernel, (shape((32, RANK)), shape((16, RANK))), (everyone, gram_link), "day_rows"
    )
    return link.T, interval_new, day_new


def solution(mesh):
    split = Mesh(mesh.devices.reshape(8, 4, 4, 2), ("z", "x", "y", "core"))
    link, intv = ("z", "x"), ("y", "core")
    return jax.shard_map(
        body,
        mesh=split,
        in_specs=(P(intv, None, link), P(intv, None), P()),
        out_specs=(P(link + intv, None), P(intv, None), P()),
        check_vma=False,
    )
```

```python
import functools

import jax
import jax.numpy as jnp
from jax import lax
from jax.experimental import pallas as pl
from jax.experimental.pallas import tpu as pltpu
from jax.sharding import Mesh, PartitionSpec as P

RANK = 64
HALF = 512
HIGH = lax.Precision.HIGHEST
F32 = jnp.float32
BF16 = jnp.bfloat16


def partners(n, d):
    return [(i, i ^ d) for i in range(n)]


def iota(shape, dim):
    return lax.broadcasted_iota(jnp.int32, shape, dim)


def dot(a, b, contract=((1,), (0,)), precision=HIGH):
    return lax.dot_general(a, b, (contract, ((), ())), precision=precision, preferred_element_type=F32)


def shifted(system):
    eye = iota((RANK, RANK), 0) == iota((RANK, RANK), 1)
    trace = jnp.sum(jnp.sum(jnp.where(eye, system, 0.0), axis=1, keepdims=True), axis=0, keepdims=True)
    return system + jnp.where(eye, 0.01 * trace / RANK, 0.0)


def eliminate(system, rhs):
    work = jnp.concatenate([system, rhs], axis=1)
    parts = [work[at : at + 8] for at in range(0, RANK, 8)]
    row = iota((8, 1), 0)
    for p in range(RANK // 8):
        rows = parts[p]
        columns = [jnp.broadcast_to(rows[:, 8 * p + j : 8 * p + j + 1], rows.shape) for j in range(8)]
        for j in range(8):
            inverse = 1.0 / columns[j][j : j + 1]
            scaled = rows[j : j + 1] * inverse
            rows = jnp.where(row == j, scaled, rows - columns[j] * scaled)
            for i in range(j + 1, 8):
                scaled = columns[i][j : j + 1] * inverse
                columns[i] = jnp.where(row == j, scaled, columns[i] - columns[j] * scaled)
        for q in range(RANK // 8):
            if q != p:
                taken = parts[q][:, 8 * p : 8 * p + 1] * rows[0:1]
                for j in range(1, 8):
                    taken = taken + parts[q][:, 8 * p + j : 8 * p + j + 1] * rows[j : j + 1]
                parts[q] = parts[q] - taken
        parts[p] = rows
    return jnp.concatenate(parts, axis=0)


def to_lanes(rows):
    return jnp.concatenate([rows[at : at + 8] for at in range(0, rows.shape[0], 8)], axis=1)


def from_lanes(wide):
    return jnp.concatenate([wide[:, at : at + RANK] for at in range(0, wide.shape[1], RANK)], axis=0)


def load_blocks(slab_ref, held_ref, sems, core):
    copies = []
    for d in range(4):
        at = pl.multiple_of((2 * (lax.axis_index("y") ^ d) + core) * 1024, 1024)
        copies.append(pltpu.make_async_copy(slab_ref.at[:, pl.ds(at, 1024)], held_ref.at[d], sems.at[d]))
        copies[-1].start()
    return copies


def send_kernel(slab_ref, interval_ref, day_ref, sums_ref, held_ref, khatri_ref, day_twice_ref, sems, *own
):
    factor, day, small_sems = own
    small = [
        pltpu.make_async_copy(interval_ref, factor, small_sems.at[0]),
        pltpu.make_async_copy(day_ref, day, small_sems.at[1]),
    ]
    for copy in small:
        copy.start()
    copies = load_blocks(slab_ref, held_ref, sems, 1 - lax.axis_index("core"))
    for copy in small:
        copy.wait()
    product = factor[...][:, None, :] * day[...][None, :, :]
    khatri = product.reshape(product.shape[0] * product.shape[1], RANK).T.astype(BF16)
    khatri_ref[...] = khatri
    sums_ref[4 * RANK :, : 4 * RANK] = to_lanes(factor[...])
    sums_ref[4 * RANK :, 4 * RANK :] = jnp.zeros((8, 1024 - 4 * RANK), F32)
    day_twice_ref[...] = jnp.concatenate([day[...], day[...]], axis=1)
    for d in range(4):
        copies[d].wait()
        sums_ref[d * RANK : (d + 1) * RANK] = dot(khatri, held_ref[d], precision=None)


def keep_kernel(slab_ref, khatri_ref, sums_ref, held_ref, sems):
    copies = load_blocks(slab_ref, held_ref, sems, lax.axis_index("core"))
    for d in range(4):
        copies[d].wait()
        sums_ref[d] = dot(khatri_ref[...], held_ref[d], precision=None)


def unpack(packed):
    return jnp.concatenate([packed[:, :RANK], packed[:, RANK:]], axis=0)


def add_kernel(keep_ref, sent_ref, got_ref, own, factor_ref, two, one_a, three_a, one_b, three_b):
    factors = [ref[4 * RANK :, : 4 * RANK] for ref in (sent_ref, got_ref)]
    factor = jnp.concatenate(factors, axis=1)
    factor_ref[...] = factor

    def total(d, lanes):
        return keep_ref[d, :, lanes] + got_ref[d * RANK : (d + 1) * RANK, lanes]

    own[...] = total(0, slice(0, 1024))
    for i in range(8):
        two[i * RANK : (i + 1) * RANK] = total(2, slice(i * 128, (i + 1) * 128))
    two[8 * RANK :] = jnp.concatenate([from_lanes(rows) for rows in factors], axis=1)
    for d, first, second in ((1, one_a, one_b), (3, three_a, three_b)):
        first[:RANK] = total(d, slice(0, HALF))
        first[RANK:] = factor
        second[...] = total(d, slice(HALF, 1024))


def inverse_kernel(own, two, one, three, day_ref, inverse_ref, gram_day_ref):
    day = day_ref[:, :RANK]
    gram_day = dot(day, day, ((0,), (0,)))
    gram_day_ref[...] = gram_day
    wide = (own[...], one[RANK:], three[RANK:])
    factor = jnp.concatenate([unpack(two[8 * RANK :])] + [from_lanes(rows) for rows in wide], axis=0)
    inverse_ref[...] = inverse_of(dot(factor, factor, ((0,), (0,))) * gram_day)


def link_kernel(own, two, one_a, three_a, one_b, inverse_ref, link_ref):
    lanes = jnp.concatenate([two[at : at + RANK] for at in range(0, 8 * RANK, RANK)], axis=1)
    first = (own[:, :HALF] + lanes[:, :HALF]) + (one_a[:RANK] + three_a[:RANK])
    second = (own[:, HALF:] + lanes[:, HALF:]) + one_b[...]
    link_ref[...] = dot(inverse_ref[...], jnp.concatenate([first, second], axis=1))


def last_link_kernel(before, three_b, inverse_ref, link_ref, low_ref):
    first = before[:, :HALF]
    second = before[:, HALF:] + dot(inverse_ref[...], three_b[...])
    link_ref[:, :HALF] = first
    link_ref[:, HALF:] = second
    low_ref[:, :HALF] = first.astype(BF16)
    low_ref[:, HALF:] = second.astype(BF16)


def times_blocks(lows, held_ref, blocks):
    total = None
    for low, i in zip(lows, blocks):
        rows = low[...]
        none = jnp.zeros_like(rows)
        for side in range(2):
            starts = range(side * RANK, 512, 2 * RANK)
            left = [held_ref[i, at : at + RANK] for at in starts] + [rows[side * 32 : side * 32 + 32]]
            right = jnp.concatenate([none, rows] if side else [rows, none], axis=0)
            term = dot(jnp.concatenate(left, axis=0), right, ((1,), (1,)), None)
            total = term if total is None else total + term
    return total


def first_partial_kernel(low, keep_ref, link_ref, acc, link_out):
    link_out[...] = link_ref[...]
    acc[...] = times_blocks((low,), keep_ref, (0,))


def second_partial_kernel(low2, low_other, keep_ref, send_ref, before, acc):
    acc[...] = before[...] + times_blocks((low2,), keep_ref, (2,)) + times_blocks((low_other,), send_ref, (0,))


def one_partial_kernel(block, low, keep_ref, before, acc):
    acc[...] = before[...] + times_blocks((low,), keep_ref, (block,))


def mixed_partial_kernel(low3, other2, other1, keep_ref, send_ref, before, acc):
    acc[...] = (
        before[...] + times_blocks((low3,), keep_ref, (3,)) + times_blocks((other2, other1), send_ref, (2, 1))
    )


def last_partial_kernel(low, send_ref, before, *refs):
    outs, acc = refs[:4], refs[4]
    acc[...] = before[...] + times_blocks((low,), send_ref, (3,))
    for d, out in enumerate(outs):
        at = pl.multiple_of((lax.axis_index("x") ^ d) * RANK, RANK)
        out[:RANK] = acc[pl.ds(at, RANK)]
        out[RANK:] = acc[4 * RANK :]


def inverse_of(system):
    eye = jnp.where(iota((RANK, RANK), 0) == iota((RANK, RANK), 1), 1.0, 0.0).astype(F32)
    return eliminate(shifted(system), eye)[:, RANK:]


def solve_rows(system, rows):
    count = rows.shape[0]
    wide = jnp.concatenate([rows, jnp.zeros((count, RANK), F32)], axis=1)
    rhs = jnp.concatenate([jnp.transpose(wide)[:RANK], jnp.zeros((RANK, RANK - count), F32)], axis=1)
    return jnp.transpose(eliminate(shifted(system), rhs))[RANK : RANK + count]


def interval_kernel(part0, part1, part2, part3, gram_day_ref, day_ref, out_ref, gram_ref):
    total = (part0[...] + part1[...]) + (part2[...] + part3[...])
    gram = unpack(total[RANK:])
    gram_ref[...] = gram
    partial = total[:RANK].reshape(4, 16, 2 * RANK)
    sums = jnp.sum(partial * day_ref[...][None], axis=1)
    rows = solve_rows(gram * gram_day_ref[...], jnp.concatenate([sums[:, :RANK], sums[:, RANK:]], axis=0))
    day_part = jnp.sum(partial * jnp.concatenate([rows[:4], rows[4:]], axis=1)[:, None, :], axis=0)
    day_part = day_part[:, :RANK] + day_part[:, RANK:]
    none = jnp.zeros((8, RANK), F32)
    out_ref[:8] = jnp.concatenate([day_part[:8], day_part[8:]], axis=1)
    out_ref[8:] = jnp.where(
        lax.axis_index("core") == 0, jnp.concatenate([rows, none], axis=1), jnp.concatenate([none, rows], axis=1)
    )


def day_kernel(recv_ref, gram_ref, interval_ref, day_ref):
    rows = recv_ref[:, 8:].reshape(8 * recv_ref.shape[0], 2 * RANK)
    gram_new = dot(rows, rows, ((0,), (0,)))
    gram_new = gram_new[:RANK, :RANK] + gram_new[RANK:, RANK:]
    total = recv_ref[0, :8]
    for i in range(1, recv_ref.shape[0]):
        total = total + recv_ref[i, :8]
    for i in range(4):
        both = recv_ref[i * 4 + lax.axis_index("y"), 8:]
        interval_ref[i * 8 : i * 8 + 8] = jnp.where(lax.axis_index("core") == 0, both[:, :RANK], both[:, RANK:])
    day_ref[...] = solve_rows(
        gram_ref[...] * gram_new, jnp.concatenate([total[:, :RANK], total[:, RANK:]], axis=0)
    )


def shape(dims, dtype=F32):
    return jax.ShapeDtypeStruct(dims, dtype)


def call(kernel, out_shape, args, name, spaces=None, scratch=()):
    spaces = spaces or {}
    return pl.pallas_call(
        kernel,
        out_shape=out_shape,
        in_specs=[pl.BlockSpec(memory_space=spaces.get(i, pltpu.VMEM)) for i in range(len(args))],
        out_specs=jax.tree.map(lambda _: pl.BlockSpec(memory_space=pltpu.VMEM), out_shape),
        scratch_shapes=scratch,
        compiler_params=pltpu.CompilerParams(vmem_limit_bytes=16 * 2**20),
        cost_estimate=pl.CostEstimate(flops=2**20, bytes_accessed=2**16, transcendentals=0),
        name=name,
    )(*args)


def body(slab, interval_factor, day_factor):
    intervals, days, links = slab.shape
    flat = pltpu.with_memory_space_constraint(slab.reshape(intervals * days, links), pltpu.HBM)
    interval_factor = pltpu.with_memory_space_constraint(interval_factor, pltpu.HBM)
    day_factor = pltpu.with_memory_space_constraint(day_factor, pltpu.HBM)
    held = shape((4, 512, 1024), BF16)

    def other_core(a):
        return lax.ppermute(a, "core", partners(2, 1))

    def along_y(a, d):
        return lax.ppermute(a, "y", partners(4, d))

    send, held_send, khatri, day_twice = call(
        send_kernel,
        (shape((264, 1024)), held, shape((RANK, 512), BF16), shape((16, 2 * RANK))),
        (flat, interval_factor, day_factor),
        "sums_to_send",
        {0: pl.ANY, 1: pl.ANY, 2: pl.ANY},
        [
            pltpu.SemaphoreType.DMA((4,)),
            pltpu.VMEM((32, RANK), F32),
            pltpu.VMEM((16, RANK), F32),
            pltpu.SemaphoreType.DMA((2,)),
        ],
    )
    got = other_core(send)
    keep, held_keep = call(
        keep_kernel,
        (shape((4, RANK, 1024)), held),
        (flat, khatri),
        "sums_to_keep",
        {0: pl.ANY},
        [pltpu.SemaphoreType.DMA((4,))],
    )
    own, factor, two, one_a, three_a, one_b, three_b = call(
        add_kernel,
        (
            shape((RANK, 1024)),
            shape((8, HALF)),
            shape((8 * RANK + 32, 128)),
            shape((72, HALF)),
            shape((72, HALF)),
            shape((RANK, HALF)),
            shape((RANK, HALF)),
        ),
        (keep, send, got),
        "add_cores",
    )
    two, one_a, three_a = along_y(two, 2), along_y(one_a, 1), along_y(three_a, 3)
    one_b, three_b = along_y(one_b, 1), along_y(three_b, 3)
    inverse, gram_day = call(
        inverse_kernel, (shape((RANK, RANK)),) * 2, (factor, two, one_a, three_a, day_twice), "link_inverse"
    )
    link = call(
        link_kernel, shape((RANK, 1024)), (own, two, one_a, three_a, one_b, inverse), "most_of_link_rows"
    )
    link, low = call(
        last_link_kernel, (shape((RANK, 1024)), shape((RANK, 1024), BF16)), (link, three_b, inverse), "link_rows"
    )
    low2, low3, low1 = [along_y(low, d) for d in (2, 3, 1)]
    total = shape((288, 2 * RANK))

    def after(one, acc):
        return lax.optimization_barrier((one, acc))[0]

    acc, link = call(
        first_partial_kernel,
        (total, shape((RANK, 1024))),
        (low, held_keep, link),
        "partial_own",
    )
    low_other = other_core(after(low, acc))
    low2 = after(low2, acc)
    other2 = other_core(low2)
    acc = call(second_partial_kernel, total, (low2, low_other, held_keep, held_send, acc), "partial_two")
    low1 = after(low1, acc)
    other1 = other_core(low1)
    acc = call(functools.partial(one_partial_kernel, 1), total, (low1, held_keep, acc), "partial_one")
    low3 = after(low3, acc)
    other3 = other_core(low3)
    acc = call(mixed_partial_kernel, total, (low3, other2, other1, held_keep, held_send, acc), "partial_mixed")
    outgoing = call(
        last_partial_kernel,
        (shape((96, 128)),) * 4,
        (other3, held_send, acc),
        "partial_last",
        None,
        [pltpu.VMEM((288, 2 * RANK), F32)],
    )
    over_x = sum([lax.ppermute(outgoing[d], "x", partners(4, d)) for d in (1, 2, 3)], outgoing[0])
    over_pair = over_x + lax.ppermute(over_x, "z", partners(8, 6))
    over_z = [over_pair] + [lax.ppermute(over_pair, "z", partners(8, d)) for d in (1, 2, 3)]
    found, gram_link = call(
        interval_kernel,
        (shape((16, 128)), shape((RANK, RANK))),
        (*over_z, gram_day, day_twice),
        "interval_rows",
    )
    found = found + other_core(found)
    everyone = lax.all_to_all(jnp.broadcast_to(found[None], (16, 16, 128)), ("x", "y"), 0, 0)
    interval_new, day_new = call(
        day_kernel, (shape((32, RANK)), shape((16, RANK))), (everyone, gram_link), "day_rows"
    )
    return link.T, interval_new, day_new


def solution(mesh):
    split = Mesh(mesh.devices.reshape(8, 4, 4, 2), ("z", "x", "y", "core"))
    link, intv = ("z", "x"), ("y", "core")
    return jax.shard_map(
        body,
        mesh=split,
        in_specs=(P(intv, None, link), P(intv, None), P()),
        out_specs=(P(link + intv, None), P(intv, None), P()),
        check_vma=False,
    )
```

```python
import functools

import jax
import jax.numpy as jnp
from jax import lax
from jax.experimental import pallas as pl
from jax.experimental.pallas import tpu as pltpu
from jax.sharding import Mesh, PartitionSpec as P

RANK = 64
HALF = 512
HIGH = lax.Precision.HIGHEST
F32 = jnp.float32
BF16 = jnp.bfloat16


def partners(n, d):
    return [(i, i ^ d) for i in range(n)]


def iota(shape, dim):
    return lax.broadcasted_iota(jnp.int32, shape, dim)


def dot(a, b, contract=((1,), (0,)), precision=HIGH):
    return lax.dot_general(a, b, (contract, ((), ())), precision=precision, preferred_element_type=F32)


def shifted(system):
    eye = iota((RANK, RANK), 0) == iota((RANK, RANK), 1)
    trace = jnp.sum(jnp.sum(jnp.where(eye, system, 0.0), axis=1, keepdims=True), axis=0, keepdims=True)
    return system + jnp.where(eye, 0.01 * trace / RANK, 0.0)


def eliminate(system, rhs):
    work = jnp.concatenate([system, rhs], axis=1)
    parts = [work[at : at + 8] for at in range(0, RANK, 8)]
    row = iota((8, 1), 0)
    for p in range(RANK // 8):
        rows = parts[p]
        columns = [jnp.broadcast_to(rows[:, 8 * p + j : 8 * p + j + 1], rows.shape) for j in range(8)]
        for j in range(8):
            inverse = 1.0 / columns[j][j : j + 1]
            scaled = rows[j : j + 1] * inverse
            rows = jnp.where(row == j, scaled, rows - columns[j] * scaled)
            for i in range(j + 1, 8):
                scaled = columns[i][j : j + 1] * inverse
                columns[i] = jnp.where(row == j, scaled, columns[i] - columns[j] * scaled)
        for q in range(RANK // 8):
            if q != p:
                taken = parts[q][:, 8 * p : 8 * p + 1] * rows[0:1]
                for j in range(1, 8):
                    taken = taken + parts[q][:, 8 * p + j : 8 * p + j + 1] * rows[j : j + 1]
                parts[q] = parts[q] - taken
        parts[p] = rows
    return jnp.concatenate(parts, axis=0)


def to_lanes(rows):
    return jnp.concatenate([rows[at : at + 8] for at in range(0, rows.shape[0], 8)], axis=1)


def from_lanes(wide):
    return jnp.concatenate([wide[:, at : at + RANK] for at in range(0, wide.shape[1], RANK)], axis=0)


def load_blocks(slab_ref, held_ref, sems, core):
    copies = []
    for d in range(4):
        at = pl.multiple_of((2 * (lax.axis_index("y") ^ d) + core) * 1024, 1024)
        copies.append(pltpu.make_async_copy(slab_ref.at[:, pl.ds(at, 1024)], held_ref.at[d], sems.at[d]))
        copies[-1].start()
    return copies


def send_kernel(slab_ref, interval_ref, day_ref, sums_ref, held_ref, khatri_ref, day_twice_ref, sems, *own
):
    factor, day, small_sems = own
    small = [
        pltpu.make_async_copy(interval_ref, factor, small_sems.at[0]),
        pltpu.make_async_copy(day_ref, day, small_sems.at[1]),
    ]
    for copy in small:
        copy.start()
    copies = load_blocks(slab_ref, held_ref, sems, 1 - lax.axis_index("core"))
    for copy in small:
        copy.wait()
    product = factor[...][:, None, :] * day[...][None, :, :]
    khatri = product.reshape(product.shape[0] * product.shape[1], RANK).T.astype(BF16)
    khatri_ref[...] = khatri
    sums_ref[4 * RANK :, : 4 * RANK] = to_lanes(factor[...])
    sums_ref[4 * RANK :, 4 * RANK :] = jnp.zeros((8, 1024 - 4 * RANK), F32)
    day_twice_ref[...] = jnp.concatenate([day[...], day[...]], axis=1)
    for d in range(4):
        copies[d].wait()
        sums_ref[d * RANK : (d + 1) * RANK] = dot(khatri, held_ref[d], precision=None)


def keep_kernel(slab_ref, khatri_ref, sums_ref, held_ref, sems):
    copies = load_blocks(slab_ref, held_ref, sems, lax.axis_index("core"))
    for d in range(4):
        copies[d].wait()
        sums_ref[d] = dot(khatri_ref[...], held_ref[d], precision=None)


def unpack(packed):
    return jnp.concatenate([packed[:, :RANK], packed[:, RANK:]], axis=0)


def add_kernel(keep_ref, sent_ref, got_ref, own, factor_ref, two, one_a, three_a, one_b, three_b):
    factors = [ref[4 * RANK :, : 4 * RANK] for ref in (sent_ref, got_ref)]
    factor = jnp.concatenate(factors, axis=1)
    factor_ref[...] = factor

    def total(d, lanes):
        return keep_ref[d, :, lanes] + got_ref[d * RANK : (d + 1) * RANK, lanes]

    own[...] = total(0, slice(0, 1024))
    for i in range(8):
        two[i * RANK : (i + 1) * RANK] = total(2, slice(i * 128, (i + 1) * 128))
    two[8 * RANK :] = jnp.concatenate([from_lanes(rows) for rows in factors], axis=1)
    for d, first, second in ((1, one_a, one_b), (3, three_a, three_b)):
        first[:RANK] = total(d, slice(0, HALF))
        first[RANK:] = factor
        second[...] = total(d, slice(HALF, 1024))


def inverse_kernel(own, two, one, three, day_ref, inverse_ref, gram_day_ref):
    day = day_ref[:, :RANK]
    gram_day = dot(day, day, ((0,), (0,)))
    gram_day_ref[...] = gram_day
    wide = (own[...], one[RANK:], three[RANK:])
    factor = jnp.concatenate([unpack(two[8 * RANK :])] + [from_lanes(rows) for rows in wide], axis=0)
    inverse_ref[...] = inverse_of(dot(factor, factor, ((0,), (0,))) * gram_day)


def link_kernel(own, two, one_a, three_a, one_b, inverse_ref, link_ref):
    lanes = jnp.concatenate([two[at : at + RANK] for at in range(0, 8 * RANK, RANK)], axis=1)
    first = (own[:, :HALF] + lanes[:, :HALF]) + (one_a[:RANK] + three_a[:RANK])
    second = (own[:, HALF:] + lanes[:, HALF:]) + one_b[...]
    link_ref[...] = dot(inverse_ref[...], jnp.concatenate([first, second], axis=1))


def last_link_kernel(before, three_b, inverse_ref, link_ref, low_ref):
    first = before[:, :HALF]
    second = before[:, HALF:] + dot(inverse_ref[...], three_b[...])
    link_ref[:, :HALF] = first
    link_ref[:, HALF:] = second
    low_ref[:, :HALF] = first.astype(BF16)
    low_ref[:, HALF:] = second.astype(BF16)


def times_blocks(lows, held_ref, blocks):
    total = None
    for low, i in zip(lows, blocks):
        rows = low[...]
        none = jnp.zeros_like(rows)
        for side in range(2):
            starts = range(side * RANK, 512, 2 * RANK)
            left = [held_ref[i, at : at + RANK] for at in starts] + [rows[side * 32 : side * 32 + 32]]
            right = jnp.concatenate([none, rows] if side else [rows, none], axis=0)
            term = dot(jnp.concatenate(left, axis=0), right, ((1,), (1,)), None)
            total = term if total is None else total + term
    return total


def first_partial_kernel(low, keep_ref, acc):
    acc[...] = times_blocks((low,), keep_ref, (0,))


def second_partial_kernel(low2, low_other, keep_ref, send_ref, before, link_ref, acc, link_out):
    link_out[...] = link_ref[...]
    acc[...] = before[...] + times_blocks((low2,), keep_ref, (2,)) + times_blocks((low_other,), send_ref, (0,))


def one_partial_kernel(block, low, keep_ref, before, acc):
    acc[...] = before[...] + times_blocks((low,), keep_ref, (block,))


def mixed_partial_kernel(low3, other2, other1, keep_ref, send_ref, before, acc):
    acc[...] = (
        before[...] + times_blocks((low3,), keep_ref, (3,)) + times_blocks((other2, other1), send_ref, (2, 1))
    )


def last_partial_kernel(low, send_ref, before, *refs):
    outs, acc = refs[:4], refs[4]
    acc[...] = before[...] + times_blocks((low,), send_ref, (3,))
    for d, out in enumerate(outs):
        at = pl.multiple_of((lax.axis_index("x") ^ d) * RANK, RANK)
        out[:RANK] = acc[pl.ds(at, RANK)]
        out[RANK:] = acc[4 * RANK :]


def inverse_of(system):
    eye = jnp.where(iota((RANK, RANK), 0) == iota((RANK, RANK), 1), 1.0, 0.0).astype(F32)
    return eliminate(shifted(system), eye)[:, RANK:]


def solve_rows(system, rows):
    count = rows.shape[0]
    wide = jnp.concatenate([rows, jnp.zeros((count, RANK), F32)], axis=1)
    rhs = jnp.concatenate([jnp.transpose(wide)[:RANK], jnp.zeros((RANK, RANK - count), F32)], axis=1)
    return jnp.transpose(eliminate(shifted(system), rhs))[RANK : RANK + count]


def interval_kernel(part0, part1, part2, part3, gram_day_ref, day_ref, out_ref, gram_ref):
    total = (part0[...] + part1[...]) + (part2[...] + part3[...])
    gram = unpack(total[RANK:])
    gram_ref[...] = gram
    partial = total[:RANK].reshape(4, 16, 2 * RANK)
    sums = jnp.sum(partial * day_ref[...][None], axis=1)
    rows = solve_rows(gram * gram_day_ref[...], jnp.concatenate([sums[:, :RANK], sums[:, RANK:]], axis=0))
    day_part = jnp.sum(partial * jnp.concatenate([rows[:4], rows[4:]], axis=1)[:, None, :], axis=0)
    day_part = day_part[:, :RANK] + day_part[:, RANK:]
    none = jnp.zeros((8, RANK), F32)
    out_ref[:8] = jnp.concatenate([day_part[:8], day_part[8:]], axis=1)
    out_ref[8:] = jnp.where(
        lax.axis_index("core") == 0, jnp.concatenate([rows, none], axis=1), jnp.concatenate([none, rows], axis=1)
    )


def day_kernel(recv_ref, gram_ref, interval_ref, day_ref):
    rows = recv_ref[:, 8:].reshape(8 * recv_ref.shape[0], 2 * RANK)
    gram_new = dot(rows, rows, ((0,), (0,)))
    gram_new = gram_new[:RANK, :RANK] + gram_new[RANK:, RANK:]
    total = recv_ref[0, :8]
    for i in range(1, recv_ref.shape[0]):
        total = total + recv_ref[i, :8]
    for i in range(4):
        both = recv_ref[i * 4 + lax.axis_index("y"), 8:]
        interval_ref[i * 8 : i * 8 + 8] = jnp.where(lax.axis_index("core") == 0, both[:, :RANK], both[:, RANK:])
    day_ref[...] = solve_rows(
        gram_ref[...] * gram_new, jnp.concatenate([total[:, :RANK], total[:, RANK:]], axis=0)
    )


def shape(dims, dtype=F32):
    return jax.ShapeDtypeStruct(dims, dtype)


def call(kernel, out_shape, args, name, spaces=None, scratch=()):
    spaces = spaces or {}
    return pl.pallas_call(
        kernel,
        out_shape=out_shape,
        in_specs=[pl.BlockSpec(memory_space=spaces.get(i, pltpu.VMEM)) for i in range(len(args))],
        out_specs=jax.tree.map(lambda _: pl.BlockSpec(memory_space=pltpu.VMEM), out_shape),
        scratch_shapes=scratch,
        compiler_params=pltpu.CompilerParams(vmem_limit_bytes=16 * 2**20),
        cost_estimate=pl.CostEstimate(flops=2**20, bytes_accessed=2**16, transcendentals=0),
        name=name,
    )(*args)


def body(slab, interval_factor, day_factor):
    intervals, days, links = slab.shape
    flat = pltpu.with_memory_space_constraint(slab.reshape(intervals * days, links), pltpu.HBM)
    interval_factor = pltpu.with_memory_space_constraint(interval_factor, pltpu.HBM)
    day_factor = pltpu.with_memory_space_constraint(day_factor, pltpu.HBM)
    held = shape((4, 512, 1024), BF16)

    def other_core(a):
        return lax.ppermute(a, "core", partners(2, 1))

    def along_y(a, d):
        return lax.ppermute(a, "y", partners(4, d))

    send, held_send, khatri, day_twice = call(
        send_kernel,
        (shape((264, 1024)), held, shape((RANK, 512), BF16), shape((16, 2 * RANK))),
        (flat, interval_factor, day_factor),
        "sums_to_send",
        {0: pl.ANY, 1: pl.ANY, 2: pl.ANY},
        [
            pltpu.SemaphoreType.DMA((4,)),
            pltpu.VMEM((32, RANK), F32),
            pltpu.VMEM((16, RANK), F32),
            pltpu.SemaphoreType.DMA((2,)),
        ],
    )
    got = other_core(send)
    keep, held_keep = call(
        keep_kernel,
        (shape((4, RANK, 1024)), held),
        (flat, khatri),
        "sums_to_keep",
        {0: pl.ANY},
        [pltpu.SemaphoreType.DMA((4,))],
    )
    own, factor, two, one_a, three_a, one_b, three_b = call(
        add_kernel,
        (
            shape((RANK, 1024)),
            shape((8, HALF)),
            shape((8 * RANK + 32, 128)),
            shape((72, HALF)),
            shape((72, HALF)),
            shape((RANK, HALF)),
            shape((RANK, HALF)),
        ),
        (keep, send, got),
        "add_cores",
    )
    two, one_a, three_a = along_y(two, 2), along_y(one_a, 1), along_y(three_a, 3)
    one_b, three_b = along_y(one_b, 1), along_y(three_b, 3)
    inverse, gram_day = call(
        inverse_kernel, (shape((RANK, RANK)),) * 2, (factor, two, one_a, three_a, day_twice), "link_inverse"
    )
    link = call(
        link_kernel, shape((RANK, 1024)), (own, two, one_a, three_a, one_b, inverse), "most_of_link_rows"
    )
    link, low = call(
        last_link_kernel, (shape((RANK, 1024)), shape((RANK, 1024), BF16)), (link, three_b, inverse), "link_rows"
    )
    low2, low3, low1 = [along_y(low, d) for d in (2, 3, 1)]
    total = shape((288, 2 * RANK))

    def after(one, acc):
        return lax.optimization_barrier((one, acc))[0]

    acc = call(first_partial_kernel, total, (low, held_keep), "partial_own")
    low_other = other_core(after(low, acc))
    low2 = after(low2, acc)
    other2 = other_core(low2)
    acc, link = call(
        second_partial_kernel,
        (total, shape((RANK, 1024))),
        (low2, low_other, held_keep, held_send, acc, link),
        "partial_two",
    )
    low1 = after(low1, acc)
    other1 = other_core(low1)
    acc = call(functools.partial(one_partial_kernel, 1), total, (low1, held_keep, acc), "partial_one")
    low3 = after(low3, acc)
    other3 = other_core(low3)
    acc = call(mixed_partial_kernel, total, (low3, other2, other1, held_keep, held_send, acc), "partial_mixed")
    outgoing = call(
        last_partial_kernel,
        (shape((96, 128)),) * 4,
        (other3, held_send, acc),
        "partial_last",
        None,
        [pltpu.VMEM((288, 2 * RANK), F32)],
    )
    over_x = sum([lax.ppermute(outgoing[d], "x", partners(4, d)) for d in (1, 2, 3)], outgoing[0])
    over_pair = over_x + lax.ppermute(over_x, "z", partners(8, 6))
    over_z = [over_pair] + [lax.ppermute(over_pair, "z", partners(8, d)) for d in (1, 2, 3)]
    found, gram_link = call(
        interval_kernel,
        (shape((16, 128)), shape((RANK, RANK))),
        (*over_z, gram_day, day_twice),
        "interval_rows",
    )
    found = found + other_core(found)
    everyone = lax.all_to_all(jnp.broadcast_to(found[None], (16, 16, 128)), ("x", "y"), 0, 0)
    interval_new, day_new = call(
        day_kernel, (shape((32, RANK)), shape((16, RANK))), (everyone, gram_link), "day_rows"
    )
    return link.T, interval_new, day_new


def solution(mesh):
    split = Mesh(mesh.devices.reshape(8, 4, 4, 2), ("z", "x", "y", "core"))
    link, intv = ("z", "x"), ("y", "core")
    return jax.shard_map(
        body,
        mesh=split,
        in_specs=(P(intv, None, link), P(intv, None), P()),
        out_specs=(P(link + intv, None), P(intv, None), P()),
        check_vma=False,
    )
```
